512 devices in a mesh: expert: 128 (over z, x, core), group: 4 (over y).
Axes of the slice: x: 4, y: 4, z: 16, core: 2. Of those that a mesh axis runs over, the one named last changes fastest.
Arguments:
- layer_in: bfloat16 [4096, 4096], P(('expert', 'group')), may hold values from -3 to 3
- norm_gain: bfloat16 [4096], replicated, may hold values from 0.25 to 1.75
- route_ids: int32 [4096, 8], P('expert'), may hold values from 0 to 127, all different within a row; in each aligned block of 32 rows (0 to 31, 32 to 63, ...) at most 4 rows name the same one
- route_logits: float32 [4096, 8], P('expert'), may hold values from -6 to 6
- gate_proj: bfloat16 [128, 768, 4096], P('expert', 'group'), may hold values from -0.09375 to 0.09375
- up_proj: bfloat16 [128, 768, 4096], P('expert', 'group'), may hold values from -0.09375 to 0.09375
- down_proj: bfloat16 [128, 768, 4096], P('expert', 'group'), may hold values from -0.21875 to 0.21875
- low_feature: bfloat16 [4096, 4096], P(('expert', 'group')), may hold values from -6 to 6
- mid_feature: bfloat16 [4096, 4096], P(('expert', 'group')), may hold values from -6 to 6
- accepted_node: int32 [512], P('expert'), may hold values from 0 to 7
- join_weight: bfloat16 [3, 4096, 4096], P(None, 'expert', 'group'), may hold values from -0.0546875 to 0.0546875
Outputs:
- layer_out: bfloat16 [4096, 4096], P(('expert', 'group'))
- joined_rows: bfloat16 [512, 4096], P('expert', 'group')
The draws below stay inside these ranges and needn't reach their ends.
Inputs may be any that keep to these rules, and one draw needn't show every extreme that they name: `route_ids`: each row names 8 different experts; in each aligned block of 32 rows (the rows of one index of expert) no expert is named by more than 4 rows, and some block reaches 4.
All inputs are finite; a program needn't handle non-finite values.
Results may differ from the reference program's by a relative error of at most 0.012.
Values may be sent and summed in bfloat16 or wider, within the bound.
No kernel may reach another device: no remote copies, remote signals or barrier semaphores. Data moves between devices by JAX's collectives and lax.ppermute only.
A program may use at most 64 MiB of HBM per device.

```python
import math
import jax
import jax.numpy as jnp
import numpy as np
from jax import lax

D = 4096
EXPERTS = 128
TOP = 8
FF = 768
FF_DEV = 192
TREE = 8
BLOCK = 32
CAP = 4
TREES = 512
TOKENS = 4096
N_GROUP = 4


def touch_ends(entries, own_key, low, top_value):
    dims = entries.shape
    spot = [jax.random.randint(jax.random.fold_in(own_key, axis), (), 0, dims[axis]) for axis in range(len(dims))]
    entries = entries.at[tuple(spot)].set(low)
    longest = dims.index(max(dims))
    spot[longest] = (spot[longest] + 1) % dims[longest]
    return entries.at[tuple(spot)].set(top_value)


def block_levels(stream_key, extent, split, least, largest):
    level = 1.0
    for axis_at, shards_of in split:
        heights = jax.random.uniform(jax.random.fold_in(jax.random.fold_in(stream_key, 6), axis_at), (shards_of,), jnp.float32, least / len(split), largest / len(split))
        level = level * jnp.repeat(jnp.exp(heights), extent[axis_at] // shards_of).reshape((-1,) + (1,) * (len(extent) - 1 - axis_at))
    return level


def routed_block(rng, own, number, rows, amount, top, bound, skew):
    ranking = jax.random.permutation(rng, amount)
    packed, ordinary = shares(amount, rows * top, bound, skew, True), shares(amount, rows * top, bound, skew, False)
    places = jnp.arange(amount)

    def named(lengths, rotation):
        used = int((lengths > 0).sum())
        fixed = max(1, used // 4)
        passed = fixed + (places - fixed + rotation * (used - fixed)) % max(1, amount - fixed)
        return jnp.zeros((amount,), jnp.int32).at[ranking[jnp.where(places < fixed, places, passed)]].set(jnp.asarray(lengths, jnp.int32))

    lengths = jnp.where(number % 4 == 0, named(packed, number // 4), named(ordinary, number - number // 4 - 1))
    mixed = jax.random.permutation(jax.random.fold_in(own, 3), amount)
    source_of, sink = mixed[0:amount // 2 * 2:2], mixed[1:amount // 2 * 2:2]
    margin = jnp.minimum(lengths[source_of] - 1, bound - lengths[sink]) // 2
    margin = jnp.where((source_of == ranking[0]) | (sink == ranking[0]) | (lengths[sink] == 0), 0, jnp.maximum(margin, 0))
    passed = jax.random.randint(jax.random.fold_in(own, 4), (amount // 2,), 0, 1 << 20) % (margin + 1)
    lengths = lengths.at[source_of].add(-passed).at[sink].add(passed)
    items = jnp.searchsorted(jnp.cumsum(lengths), jnp.arange(rows * top), side="right").astype(jnp.int32)
    listing = items.reshape(top, rows).T
    listing = listing[jax.random.permutation(jax.random.fold_in(own, 1), rows)]
    rotation = jax.random.randint(jax.random.fold_in(own, 2), (rows, 1), 0, top)
    return jnp.take_along_axis(listing, (jnp.arange(top)[None, :] + rotation) % top, axis=1)


def shares(number_of, total, bound, lean, full):
    loads = [(1 << 20) // math.isqrt(rank ** lean) + 1 for rank in range(1, number_of + 1)]
    largest = bound if full else min(bound, max(-(-total // number_of), total * loads[0] // sum(loads)))
    least = 1 if total - largest >= number_of - 1 else 0
    holding, spare = [largest] + [least] * (number_of - 1), total - largest - least * (number_of - 1)
    while spare > 0:
        candidates = [i for i in range(1, number_of) if holding[i] < largest] or [i for i in range(1, number_of) if holding[i] < bound]
        pool, left = sum([loads[i] for i in candidates]), spare
        for i in candidates:
            extra = min(bound - holding[i], max(1, left * loads[i] // pool), spare)
            holding[i] = holding[i] + extra
            spare = spare - extra
    return np.array(holding)


def gaussian(key, extent, scale, limit, shards=(), held_as=jnp.bfloat16):
    loudness = block_levels(key, extent, shards, -0.22, 0.18) if shards else 1.0
    values = jax.random.normal(key, extent, jnp.float32) * scale * loudness
    return jnp.minimum(jnp.maximum(values, -limit), limit).astype(held_as)


def setup_inputs(seed: int = 0) -> dict:
    key_list = jax.random.split(jax.random.key(seed), 12)
    layer_in = gaussian(key_list[0], (TOKENS, D), 0.5, 3.0, ((0, 512),))
    norm_gain = jnp.clip(1.0 + 0.15 * jax.random.normal(key_list[1], (D,), jnp.float32), 0.25, 1.75).astype(jnp.bfloat16)
    route_ids_keys = jax.random.split(jax.random.fold_in(key_list[2], 1), TOKENS // BLOCK)
    route_ids_turns = jax.random.permutation(jax.random.fold_in(key_list[2], 3), TOKENS // BLOCK)
    route_ids = jax.vmap(lambda own, number: routed_block(jax.random.fold_in(key_list[2], 2), own, number, BLOCK, EXPERTS, TOP, CAP, 2))(route_ids_keys, route_ids_turns).reshape((TOKENS, TOP))
    route_logits = gaussian(key_list[3], (TOKENS, TOP), 1.5, 6.0, ((0, 128),), jnp.float32)
    gate_proj = gaussian(key_list[4], (EXPERTS, FF, D), D ** -0.5, 0.09375, ((0, 128), (1, 4)))
    up_proj = gaussian(key_list[5], (EXPERTS, FF, D), D ** -0.5, 0.09375, ((0, 128), (1, 4)))
    down_proj = gaussian(key_list[6], (EXPERTS, FF, D), FF ** -0.5, 0.21875, ((0, 128), (1, 4)))
    low_feature = gaussian(key_list[7], (TOKENS, D), 1.0, 6.0, ((0, 512),))
    mid_feature = gaussian(key_list[8], (TOKENS, D), 1.0, 6.0, ((0, 512),))
    accepted_node = touch_ends(jax.random.randint(key_list[9], (TREES,), 0, TREE), jax.random.fold_in(key_list[9], 1), 0, TREE - 1).astype(jnp.int32)
    join_weight = gaussian(key_list[10], (3, D, D), (3 * D) ** -0.5, 0.0546875, ((1, 128), (2, 4)))
    return {"layer_in": layer_in, "norm_gain": norm_gain, "route_ids": route_ids, "route_logits": route_logits, "gate_proj": gate_proj, "up_proj": up_proj, "down_proj": down_proj, "low_feature": low_feature, "mid_feature": mid_feature, "accepted_node": accepted_node, "join_weight": join_weight}


EPSILON = 1e-06

def rms_norm(values, norm_gain):
    widened = values.astype(jnp.float32)
    inverse_rms = lax.rsqrt(lax.optimization_barrier(jnp.mean(widened * widened, axis=-1, keepdims=True)) + EPSILON)
    return (widened * inverse_rms * norm_gain.astype(jnp.float32)).astype(jnp.bfloat16)

def route_weights(route_logits):
    exponent = jnp.exp(route_logits.astype(jnp.float32))
    return (exponent / lax.optimization_barrier(jnp.sum(exponent, axis=-1, keepdims=True))).astype(jnp.bfloat16)

def slot_rank(route_block, experts):
    flat_ids = route_block.reshape(-1)
    columns = jnp.arange(experts, dtype=jnp.int32)
    onehot = (flat_ids[:, None] == columns[None, :]).astype(jnp.int32)
    before = jnp.cumsum(onehot, axis=0) - onehot
    return lax.optimization_barrier(jnp.sum(before * onehot, axis=1)).reshape(route_block.shape).astype(jnp.int32)

def reference(layer_in, norm_gain, route_ids, route_logits, gate_proj, up_proj, down_proj, low_feature, mid_feature, accepted_node, join_weight):
    token_count, model_width = layer_in.shape
    experts = gate_proj.shape[0]
    normed = rms_norm(layer_in, norm_gain)
    weights = route_weights(route_logits)
    blocks = token_count // BLOCK
    ranked = jax.vmap(lambda route_block: slot_rank(route_block, experts))(route_ids.reshape(blocks, BLOCK, TOP))
    ranked = ranked.reshape(token_count, TOP)
    block_of = (jnp.arange(token_count, dtype=jnp.int32) // BLOCK)[:, None]
    slot_place = (block_of * CAP + ranked).astype(jnp.int32)
    token_of = jnp.broadcast_to(jnp.arange(token_count, dtype=jnp.int32)[:, None], (token_count, TOP))
    token_table = jnp.full((experts, blocks * CAP), token_count, jnp.int32).at[route_ids, slot_place].set(token_of)
    weight_table = jnp.zeros((experts, blocks * CAP), jnp.bfloat16).at[route_ids, slot_place].set(weights)
    padded = jnp.concatenate([normed, jnp.zeros((1, model_width), jnp.bfloat16)], axis=0)

    def one_expert(summed, inputs):
        w_gate, w_up, w_down, table_rows, scales = inputs
        picked = padded[table_rows]
        gate_act = jnp.dot(picked, w_gate.T, preferred_element_type=jnp.float32)
        up_act = jnp.dot(picked, w_up.T, preferred_element_type=jnp.float32)
        hidden = (jax.nn.silu(gate_act) * up_act).astype(jnp.bfloat16)
        result = jnp.zeros((table_rows.shape[0], model_width), jnp.float32)
        for slice_index in range(N_GROUP):
            lower = slice_index * FF_DEV
            piece_out = jnp.dot(hidden[:, lower:lower + FF_DEV], w_down[lower:lower + FF_DEV], preferred_element_type=jnp.float32).astype(jnp.bfloat16)
            result = result + scales.astype(jnp.float32)[:, None] * piece_out.astype(jnp.float32)
        return (summed.at[table_rows].add(result), None)
    summed, _ = lax.scan(one_expert, jnp.zeros((token_count + 1, model_width), jnp.float32), (gate_proj, up_proj, down_proj, token_table, weight_table))
    layer_out = (layer_in.astype(jnp.float32) + summed[:token_count]).astype(jnp.bfloat16)
    tree_count = accepted_node.shape[0]
    chosen = (jnp.arange(tree_count, dtype=jnp.int32) * TREE + accepted_node).astype(jnp.int32)
    joined = jnp.dot(low_feature[chosen], join_weight[0], preferred_element_type=jnp.float32)
    joined = joined + jnp.dot(mid_feature[chosen], join_weight[1], preferred_element_type=jnp.float32)
    joined = joined + jnp.dot(layer_out[chosen], join_weight[2], preferred_element_type=jnp.float32)
    return (layer_out, joined.astype(jnp.bfloat16))
```

```python
import jax
import jax.numpy as jnp
from jax import lax
from jax.sharding import Mesh
from jax.sharding import PartitionSpec as P

EPSILON = 1e-06
Z_SIZE = 16
P_SIZE = 8
CAP = 4
EXPERT = ("z", "p")
F32 = jnp.float32
BF16 = jnp.bfloat16


def rms_norm(values, norm_gain):
    widened = values.astype(F32)
    inverse_rms = lax.rsqrt(jnp.mean(widened * widened, axis=-1, keepdims=True) + EPSILON)
    return (widened * inverse_rms * norm_gain.astype(F32)).astype(BF16)


def route_weights(route_logits):
    exponent = jnp.exp(route_logits)
    return (exponent / jnp.sum(exponent, axis=-1, keepdims=True)).astype(BF16)


def slot_places(route_ids, experts):
    flat_ids = route_ids.reshape(-1)
    amount = flat_ids.shape[0]
    onehot = flat_ids[:, None] == jnp.arange(experts, dtype=jnp.int32)[None, :]
    lower = jnp.arange(amount)[:, None] > jnp.arange(amount)[None, :]
    before = jnp.dot(lower.astype(BF16), onehot.astype(BF16), preferred_element_type=F32)
    rank = jnp.sum(jnp.where(onehot, before, 0.0), axis=1).astype(jnp.int32)
    return flat_ids * CAP + rank


def dot_t(rows, weight):
    return lax.dot_general(rows, weight, (((1,), (1,)), ((), ())), preferred_element_type=F32)


def shift_y(array, groups, shift):
    return lax.ppermute(array, "y", [(j, (j + shift) % groups) for j in range(groups)])


def on_device(
    layer_in,
    norm_gain,
    route_ids,
    route_logits,
    gate_proj,
    up_proj,
    down_proj,
    low_feature,
    mid_feature,
    accepted_node,
    join_weight,
):
    groups = lax.axis_size("y")
    experts = Z_SIZE * P_SIZE
    g = lax.axis_index("y")
    rows_dev, width = layer_in.shape
    block, top = route_ids.shape
    part = width // groups
    slots = experts * CAP
    trees = accepted_node.shape[0]

    join_all = lax.all_gather(join_weight, "z", axis=0, tiled=False)
    join_all = join_all.reshape(-1, join_weight.shape[-1])

    stacked = jnp.concatenate([gate_proj, up_proj, down_proj], axis=0)
    pieces = []
    for s in range(groups):
        to = (g + s) % groups
        piece = lax.dynamic_slice_in_dim(stacked, to * part, part, 2)
        pieces.append(shift_y(piece, groups, s) if s else piece)

    normed_own = rms_norm(layer_in, norm_gain)
    both = jnp.stack([normed_own, layer_in], axis=0).reshape(2, rows_dev, groups, part)
    both = lax.all_to_all(both.transpose(2, 0, 1, 3), "y", 0, 0, tiled=True)
    normed = both[:, 0].reshape(block, part)
    block_in = both[:, 1].reshape(block, part)

    weights = route_weights(route_logits)
    places = slot_places(route_ids, experts)
    slot_ids = jnp.arange(slots, dtype=jnp.int32)
    matches = (places[:, None] == slot_ids[None, :]).reshape(block, top, slots)
    dispatch = jnp.any(matches, axis=1).astype(BF16)
    combine = jnp.sum(
        jnp.where(matches, weights.astype(F32)[:, :, None], 0.0), axis=1
    ).astype(BF16)

    outgoing = lax.dot_general(
        dispatch, normed, (((0,), (0,)), ((), ())), preferred_element_type=F32
    ).astype(BF16)
    received = lax.all_to_all(outgoing.reshape(experts, CAP, part), EXPERT, 0, 0, tiled=True)
    rows = received.reshape(slots, part)

    acts = None
    for s in range(groups):
        gate_up = pieces[s][:2].reshape(-1, part)
        product = dot_t(rows, gate_up)
        if s:
            product = shift_y(product.astype(BF16), groups, groups - s).astype(F32)
        acts = product if acts is None else acts + product
    units = acts.shape[1] // 2
    hidden = (jax.nn.silu(acts[:, :units]) * acts[:, units:]).astype(BF16)
    hidden_all = lax.all_gather(hidden, "y", axis=0, tiled=False)

    expert_out = None
    for s in range(groups):
        taken = lax.dynamic_index_in_dim(hidden_all, (g + groups - s) % groups, 0, keepdims=False)
        product = jnp.dot(taken, pieces[s][2], preferred_element_type=F32)
        expert_out = product if expert_out is None else expert_out + product
    expert_out = expert_out.astype(BF16).reshape(experts, CAP, part)
    returned = lax.all_to_all(expert_out, EXPERT, 0, 0, tiled=True)
    moe = jnp.dot(combine, returned.reshape(slots, part), preferred_element_type=F32)
    block_out = (block_in.astype(F32) + moe).astype(BF16)

    own_rows = lax.all_to_all(block_out.reshape(groups, rows_dev, part), "y", 0, 0, tiled=True)
    layer_out = own_rows.transpose(1, 0, 2).reshape(rows_dev, width)

    tree = rows_dev
    high = jnp.take_along_axis(
        block_out.reshape(trees, tree, part), accepted_node[:, None, None], axis=1
    )[:, 0]
    own_node = lax.dynamic_slice_in_dim(accepted_node, g, 1, 0)[0]
    low = lax.dynamic_index_in_dim(low_feature, own_node, 0, keepdims=False)
    mid = lax.dynamic_index_in_dim(mid_feature, own_node, 0, keepdims=False)
    z_part = Z_SIZE // groups
    feat = width // experts
    high = high.reshape(trees, z_part, P_SIZE, feat).transpose(2, 0, 1, 3).reshape(P_SIZE, -1)
    low = low.reshape(Z_SIZE, P_SIZE, feat).transpose(1, 0, 2).reshape(P_SIZE, -1)
    mid = mid.reshape(Z_SIZE, P_SIZE, feat).transpose(1, 0, 2).reshape(P_SIZE, -1)
    payload = jnp.stack([low, mid, high], axis=1)
    payload = jnp.broadcast_to(payload[:, None], (P_SIZE, groups) + payload.shape[1:])
    payload = payload.reshape((P_SIZE * groups,) + payload.shape[2:])
    spread = lax.all_to_all(payload, ("p", "y"), 0, 0, tiled=True)
    low_rows = spread[:, 0].reshape(P_SIZE * trees, Z_SIZE, feat)
    mid_rows = spread[:, 1].reshape(P_SIZE * trees, Z_SIZE, feat)
    high_rows = spread[:, 2].reshape(P_SIZE, groups, trees, z_part, feat)
    high_rows = high_rows.transpose(0, 2, 1, 3, 4).reshape(P_SIZE * trees, Z_SIZE, feat)
    features = jnp.stack([low_rows, mid_rows, high_rows], axis=2).reshape(P_SIZE * trees, -1)
    summed = jnp.dot(features, join_all, preferred_element_type=F32)
    summed = lax.all_to_all(summed.reshape(P_SIZE, trees, -1), "p", 0, 0, tiled=True)
    joined_rows = jnp.sum(summed, axis=0).astype(BF16)
    return (layer_out, joined_rows)


def solution(mesh):
    split = Mesh(mesh.devices.reshape(Z_SIZE, P_SIZE, -1), ("z", "p", "y"))
    every = ("z", "p", "y")
    placed = (
        P(every, None),
        P(),
        P(EXPERT, None),
        P(EXPERT, None),
        P(EXPERT, "y", None),
        P(EXPERT, "y", None),
        P(EXPERT, "y", None),
        P(every, None),
        P(every, None),
        P(EXPERT),
        P(None, EXPERT, "y"),
    )
    return jax.shard_map(
        on_device,
        mesh=split,
        in_specs=placed,
        out_specs=(P(every, None), P(EXPERT, "y")),
        check_vma=False,
    )
```

```python
import functools

import jax
import jax.numpy as jnp
from jax import lax
from jax.experimental import pallas as pl
from jax.experimental.pallas import tpu as pltpu
from jax.sharding import Mesh
from jax.sharding import PartitionSpec as P

EPSILON = 1e-06
Z_SIZE = 16
P_SIZE = 8
CAP = 4
EXPERT = ("z", "p")
F32 = jnp.float32
BF16 = jnp.bfloat16
PARAMS = pltpu.CompilerParams(vmem_limit_bytes=40 * 1024 * 1024)
VMEM = pl.BlockSpec(memory_space=pltpu.VMEM)
SMEM = pl.BlockSpec(memory_space=pltpu.SMEM)


def cost(flops, moved):
    return pl.CostEstimate(flops=flops, bytes_accessed=moved, transcendentals=0)


def norm_kernel(layer_ref, gain_ref, out_ref):
    groups, _, _, part = out_ref.shape
    widened = layer_ref[...].astype(F32)
    inverse = lax.rsqrt(jnp.mean(widened * widened, axis=-1, keepdims=True) + EPSILON)
    normed = (widened * inverse * gain_ref[...].astype(F32)).astype(BF16)
    for j in range(groups):
        out_ref[j, 0] = normed[:, j * part : (j + 1) * part]
        out_ref[j, 1] = layer_ref[:, j * part : (j + 1) * part]


def normed_and_raw(layer_in, norm_gain, groups):
    rows, width = layer_in.shape
    return pl.pallas_call(
        norm_kernel,
        out_shape=jax.ShapeDtypeStruct((groups, 2, rows, width // groups), BF16),
        in_specs=[VMEM] * 2,
        out_specs=VMEM,
        compiler_params=PARAMS,
        cost_estimate=cost(rows * width * 6, rows * width * 6),
        name="norm_pack",
    )(layer_in, norm_gain.reshape(1, width))


def slice_kernel(groups, g_ref, gate_ref, up_ref, down_ref, *refs):
    outs, sems = refs[:-1], refs[-1]
    units = gate_ref.shape[1]
    part = gate_ref.shape[2] // groups
    copies = []
    for s in range(1, groups):
        lane = pl.multiple_of(lax.rem(g_ref[0] + s, groups) * part, part)
        for k, source in enumerate((gate_ref, up_ref, down_ref)):
            copies.append(
                pltpu.make_async_copy(
                    source.at[0, :, pl.ds(lane, part)],
                    outs[s - 1].at[pl.ds(k * units, units), :],
                    sems.at[s - 1, k],
                )
            )
    for copy in copies:
        copy.start()
    for copy in copies:
        copy.wait()


def weight_pieces(g, gate, up, down, groups):
    _, units, width = gate.shape
    any_space = pl.BlockSpec(memory_space=pl.ANY)
    shape = jax.ShapeDtypeStruct((3 * units, width // groups), BF16)
    return pl.pallas_call(
        functools.partial(slice_kernel, groups),
        out_shape=[shape] * (groups - 1),
        in_specs=[SMEM] + [any_space] * 3,
        out_specs=[any_space] * (groups - 1),
        scratch_shapes=[pltpu.SemaphoreType.DMA((groups - 1, 3))],
        compiler_params=PARAMS,
        cost_estimate=cost(0, 6 * units * width * 2),
        name="weight_slices",
    )(g, gate, up, down)


def dot_nt(a, b):
    return lax.dot_general(a, b, (((1,), (1,)), ((), ())), preferred_element_type=F32)


def dot_tn(a, b):
    return lax.dot_general(a, b, (((0,), (0,)), ((), ())), preferred_element_type=F32)


def gate_up_kernel(groups, g_ref, rows_ref, gate_ref, up_ref, *refs):
    pieces, out_ref = refs[:-1], refs[-1]
    units = gate_ref.shape[1]
    rows = rows_ref[...]
    g = g_ref[0]
    out_ref[g, :units] = dot_nt(gate_ref[0], rows).astype(BF16)
    out_ref[g, units:] = dot_nt(up_ref[0], rows).astype(BF16)
    for s in range(1, groups):
        home = lax.rem(g + groups - s, groups)
        out_ref[home] = dot_nt(pieces[s - 1][...], rows).astype(BF16)


def gate_up(g, rows, gate, up, pieces, groups):
    slots, part = rows.shape
    units = gate.shape[1]
    own = pl.BlockSpec((1, units, part), lambda i, g_ref: (0, 0, g_ref[0]))
    return pl.pallas_call(
        functools.partial(gate_up_kernel, groups),
        out_shape=jax.ShapeDtypeStruct((groups, 2 * units, slots), BF16),
        grid_spec=pltpu.PrefetchScalarGridSpec(
            num_scalar_prefetch=1,
            grid=(1,),
            in_specs=[pl.BlockSpec((slots, part), lambda i, g_ref: (0, 0)), own, own]
            + [pl.BlockSpec((2 * units, part), lambda i, g_ref: (0, 0))] * (groups - 1),
            out_specs=pl.BlockSpec((groups, 2 * units, slots), lambda i, g_ref: (0, 0, 0)),
        ),
        compiler_params=PARAMS,
        cost_estimate=cost(2 * slots * part * 2 * units * groups, 6 << 20),
        name="gate_up",
    )(g, rows, gate, up, *pieces)


def silu_kernel(acts_ref, out_ref):
    units = out_ref.shape[0]
    gate = jnp.sum(acts_ref[:, :units].astype(F32), axis=0)
    up = jnp.sum(acts_ref[:, units:].astype(F32), axis=0)
    out_ref[...] = (gate / (1.0 + jnp.exp(-gate)) * up).astype(BF16)


def silu(acts):
    _, double, slots = acts.shape
    return pl.pallas_call(
        silu_kernel,
        out_shape=jax.ShapeDtypeStruct((double // 2, slots), BF16),
        in_specs=[VMEM],
        out_specs=VMEM,
        compiler_params=PARAMS,
        cost_estimate=cost(8 * double * slots, 2 << 20),
        name="silu_sum",
    )(acts)


def down_kernel(groups, g_ref, hidden_ref, own_ref, *refs):
    pieces, out_ref = refs[:-1], refs[-1]
    units = own_ref.shape[1]
    part = out_ref.shape[1]
    g = g_ref[0]
    chunk = part // 4
    held = [
        hidden_ref[pl.ds(pl.multiple_of(lax.rem(g + groups - s, groups) * units, units), units), :]
        for s in range(groups)
    ]
    for n in range(4):
        columns = slice(n * chunk, (n + 1) * chunk)
        total = dot_tn(held[0], own_ref[0, :, columns])
        for s in range(1, groups):
            total += dot_tn(held[s], pieces[s - 1][:, columns])
        out_ref[:, columns] = total.astype(BF16)


def down(g, hidden, own, pieces, groups):
    inner, slots = hidden.shape
    units = own.shape[1]
    part = own.shape[2] // groups
    return pl.pallas_call(
        functools.partial(down_kernel, groups),
        out_shape=jax.ShapeDtypeStruct((slots, part), BF16),
        grid_spec=pltpu.PrefetchScalarGridSpec(
            num_scalar_prefetch=1,
            grid=(1,),
            in_specs=[
                pl.BlockSpec((inner, slots), lambda i, g_ref: (0, 0)),
                pl.BlockSpec((1, units, part), lambda i, g_ref: (0, 0, g_ref[0])),
            ]
            + [pl.BlockSpec((units, part), lambda i, g_ref: (2, 0))] * (groups - 1),
            out_specs=pl.BlockSpec((slots, part), lambda i, g_ref: (0, 0)),
        ),
        compiler_params=PARAMS,
        cost_estimate=cost(2 * slots * inner * part, 4 << 20),
        name="down",
    )(g, hidden, own, *pieces)


def combine_kernel(node_ref, table_ref, returned_ref, block_ref, out_ref, high_ref):
    trees = high_ref.shape[0]
    tree = out_ref.shape[0] // trees
    moe = jnp.dot(table_ref[...], returned_ref[...], preferred_element_type=F32)
    result = (block_ref[...].astype(F32) + moe).astype(BF16)
    out_ref[...] = result
    widened = result.astype(F32)
    place = lax.broadcasted_iota(jnp.int32, (tree, out_ref.shape[1]), 0)
    for t in range(trees):
        rows = widened[t * tree : (t + 1) * tree]
        kept = jnp.sum(jnp.where(place == node_ref[t], rows, 0.0), axis=0, keepdims=True)
        high_ref[t : t + 1, :] = kept


def combine(nodes, table, returned, block_in):
    block, part = block_in.shape
    return pl.pallas_call(
        combine_kernel,
        out_shape=[
            jax.ShapeDtypeStruct((block, part), BF16),
            jax.ShapeDtypeStruct((nodes.shape[0], part), F32),
        ],
        in_specs=[SMEM] + [VMEM] * 3,
        out_specs=[VMEM] * 2,
        compiler_params=PARAMS,
        cost_estimate=cost(2 * block * returned.shape[0] * part, 2 << 20),
        name="combine",
    )(nodes, table, returned, block_in)


def early_kernel(rows_ref, weight_ref, out_ref):
    out_ref[...] = jnp.dot(
        rows_ref[...], weight_ref[...].reshape(-1, out_ref.shape[1]), preferred_element_type=F32
    )


def early_join(rows, weight):
    z_size, _, feat, width = weight.shape
    return pl.pallas_call(
        early_kernel,
        out_shape=jax.ShapeDtypeStruct((rows.shape[0], width), F32),
        grid=(1,),
        in_specs=[
            pl.BlockSpec(rows.shape, lambda i: (0, 0)),
            pl.BlockSpec((z_size, 2, feat, width), lambda i: (0, 0, 0, 0)),
        ],
        out_specs=pl.BlockSpec((rows.shape[0], width), lambda i: (0, 0)),
        compiler_params=PARAMS,
        cost_estimate=cost(2 * rows.shape[0] * rows.shape[1] * width, 2 << 20),
        name="join_early",
    )(rows, weight)


def late_kernel(rows_ref, weight_ref, early_ref, out_ref):
    out_ref[...] = early_ref[...] + jnp.dot(
        rows_ref[...], weight_ref[...].reshape(-1, out_ref.shape[1]), preferred_element_type=F32
    )


def late_join(rows, weight, early):
    z_size, _, feat, width = weight.shape
    return pl.pallas_call(
        late_kernel,
        out_shape=jax.ShapeDtypeStruct((rows.shape[0], width), F32),
        grid=(1,),
        in_specs=[
            pl.BlockSpec(rows.shape, lambda i: (0, 0)),
            pl.BlockSpec((z_size, 1, feat, width), lambda i: (0, 2, 0, 0)),
            pl.BlockSpec(early.shape, lambda i: (0, 0)),
        ],
        out_specs=pl.BlockSpec((rows.shape[0], width), lambda i: (0, 0)),
        compiler_params=PARAMS,
        cost_estimate=cost(2 * rows.shape[0] * rows.shape[1] * width, 1 << 20),
        name="join_late",
    )(rows, weight, early)


def route_weights(route_logits):
    exponent = jnp.exp(route_logits)
    return (exponent / jnp.sum(exponent, axis=-1, keepdims=True)).astype(BF16)


def slot_places(route_ids, experts):
    flat_ids = route_ids.reshape(-1)
    amount = flat_ids.shape[0]
    onehot = flat_ids[:, None] == jnp.arange(experts, dtype=jnp.int32)[None, :]
    lower = jnp.arange(amount)[:, None] > jnp.arange(amount)[None, :]
    before = jnp.dot(lower.astype(BF16), onehot.astype(BF16), preferred_element_type=F32)
    rank = jnp.sum(jnp.where(onehot, before, 0.0), axis=1).astype(jnp.int32)
    return flat_ids * CAP + rank


def on_device(
    layer_in,
    norm_gain,
    route_ids,
    route_logits,
    gate_proj,
    up_proj,
    down_proj,
    low_feature,
    mid_feature,
    accepted_node,
    join_weight,
):
    groups = lax.axis_size("y")
    experts = Z_SIZE * P_SIZE
    g = lax.axis_index("y").astype(jnp.int32)
    g_one = g.reshape(1)
    rows_dev, width = layer_in.shape
    block, top = route_ids.shape
    part = width // groups
    slots = experts * CAP
    trees = accepted_node.shape[0]

    join_all = lax.all_gather(join_weight, "z", axis=0, tiled=False)

    both = normed_and_raw(layer_in, norm_gain, groups)
    both = lax.all_to_all(both, "y", 0, 0, tiled=True)
    normed = both[:, 0].reshape(block, part)
    block_in = both[:, 1].reshape(block, part)

    weights = route_weights(route_logits)
    places = slot_places(route_ids, experts)
    slot_ids = jnp.arange(slots, dtype=jnp.int32)
    matches = (places[:, None] == slot_ids[None, :]).reshape(block, top, slots)
    dispatch = jnp.any(matches, axis=1).astype(BF16)
    outgoing = dot_tn(dispatch, normed).astype(BF16).reshape(experts, CAP, part)

    cut = weight_pieces(g_one, gate_proj, up_proj, down_proj, groups)
    outgoing, *cut = lax.optimization_barrier((outgoing, *cut))
    pieces = [
        lax.ppermute(piece, "y", [(j, (j + s + 1) % groups) for j in range(groups)])
        for s, piece in enumerate(cut)
    ]
    received = lax.all_to_all(outgoing, EXPERT, 0, 0, tiled=True)
    rows = received.reshape(slots, part)

    combine_table = jnp.sum(
        jnp.where(matches, weights.astype(F32)[:, :, None], 0.0), axis=1
    ).astype(BF16)

    acts = gate_up(g_one, rows, gate_proj, up_proj, pieces, groups)
    acts = lax.all_to_all(acts, "y", 0, 0, tiled=True)
    hidden = silu(acts)
    hidden_all = lax.all_gather(hidden, "y", axis=0, tiled=True)
    expert_out = down(g_one, hidden_all, down_proj, pieces, groups)
    returned = lax.all_to_all(expert_out.reshape(experts, CAP, part), EXPERT, 0, 0, tiled=True)

    own_node = lax.dynamic_slice_in_dim(accepted_node, g, 1, 0)[0]
    feat = width // experts
    low = lax.dynamic_index_in_dim(low_feature, own_node, 0, keepdims=False)
    mid = lax.dynamic_index_in_dim(mid_feature, own_node, 0, keepdims=False)
    known = jnp.stack([low.reshape(Z_SIZE, P_SIZE, feat), mid.reshape(Z_SIZE, P_SIZE, feat)], 0)
    known = known.transpose(2, 1, 0, 3).reshape(P_SIZE, 1, 1, -1)
    known = jnp.broadcast_to(known, (P_SIZE, groups, 1, known.shape[-1]))
    known = known.reshape(P_SIZE * groups, 1, -1)
    known, _ = lax.optimization_barrier((known, hidden))
    known = lax.all_to_all(known, ("p", "y"), 0, 0, tiled=True)
    early = early_join(known.reshape(P_SIZE * trees, -1), join_all)
    returned, early = lax.optimization_barrier((returned, early))

    block_out, high = combine(
        accepted_node, combine_table, returned.reshape(slots, part), block_in
    )

    z_part = Z_SIZE // groups
    high = high.astype(BF16).reshape(trees, z_part, P_SIZE, feat).transpose(2, 0, 1, 3)
    high = jnp.broadcast_to(
        high.reshape(P_SIZE, 1, trees, z_part * feat), (P_SIZE, groups, trees, z_part * feat)
    )
    high = lax.all_to_all(
        high.reshape(P_SIZE * groups, trees, z_part * feat), ("p", "y"), 0, 0, tiled=True
    )
    high = high.reshape(P_SIZE, groups, trees, z_part * feat).transpose(0, 2, 1, 3)
    summed = late_join(high.reshape(P_SIZE * trees, -1), join_all, early)
    summed = lax.all_to_all(summed.reshape(P_SIZE, trees, -1), "p", 0, 0, tiled=True)
    joined_rows = jnp.sum(summed, axis=0).astype(BF16)

    own_rows = lax.all_to_all(block_out.reshape(groups, rows_dev, part), "y", 0, 0, tiled=True)
    layer_out = own_rows.transpose(1, 0, 2).reshape(rows_dev, width)
    return (layer_out, joined_rows)


def solution(mesh):
    split = Mesh(mesh.devices.reshape(Z_SIZE, P_SIZE, -1), ("z", "p", "y"))
    every = ("z", "p", "y")
    placed = (
        P(every, None),
        P(),
        P(EXPERT, None),
        P(EXPERT, None),
        P(EXPERT, "y", None),
        P(EXPERT, "y", None),
        P(EXPERT, "y", None),
        P(every, None),
        P(every, None),
        P(EXPERT),
        P(None, EXPERT, "y"),
    )
    return jax.shard_map(
        on_device,
        mesh=split,
        in_specs=placed,
        out_specs=(P(every, None), P(EXPERT, "y")),
        check_vma=False,
    )
```

```python
import functools

import jax
import jax.numpy as jnp
from jax import lax
from jax.experimental import pallas as pl
from jax.experimental.pallas import tpu as pltpu
from jax.sharding import Mesh
from jax.sharding import PartitionSpec as P

EPSILON = 1e-06
Z_SIZE = 16
P_SIZE = 8
CAP = 4
EXPERT = ("z", "p")
F32 = jnp.float32
BF16 = jnp.bfloat16
PARAMS = pltpu.CompilerParams(vmem_limit_bytes=40 * 1024 * 1024)
VMEM = pl.BlockSpec(memory_space=pltpu.VMEM)
SMEM = pl.BlockSpec(memory_space=pltpu.SMEM)


def cost(flops, moved):
    return pl.CostEstimate(flops=flops, bytes_accessed=moved, transcendentals=0)


def norm_kernel(layer_ref, gain_ref, out_ref):
    groups, _, _, part = out_ref.shape
    widened = layer_ref[...].astype(F32)
    inverse = lax.rsqrt(jnp.mean(widened * widened, axis=-1, keepdims=True) + EPSILON)
    normed = (widened * inverse * gain_ref[...].astype(F32)).astype(BF16)
    for j in range(groups):
        out_ref[j, 0] = normed[:, j * part : (j + 1) * part]
        out_ref[j, 1] = layer_ref[:, j * part : (j + 1) * part]


def normed_and_raw(layer_in, norm_gain, groups):
    rows, width = layer_in.shape
    return pl.pallas_call(
        norm_kernel,
        out_shape=jax.ShapeDtypeStruct((groups, 2, rows, width // groups), BF16),
        in_specs=[VMEM] * 2,
        out_specs=VMEM,
        compiler_params=PARAMS,
        cost_estimate=cost(rows * width * 6, rows * width * 6),
        name="norm_pack",
    )(layer_in, norm_gain.reshape(1, width))


def slice_kernel(groups, g_ref, gate_ref, up_ref, down_ref, *refs):
    outs, sems = refs[:-1], refs[-1]
    units = gate_ref.shape[1]
    part = gate_ref.shape[2] // groups
    copies = []
    for s in range(groups):
        lane = pl.multiple_of(lax.rem(g_ref[0] + s, groups) * part, part)
        for k, source in enumerate((gate_ref, up_ref, down_ref)):
            copies.append(
                pltpu.make_async_copy(
                    source.at[0, :, pl.ds(lane, part)],
                    outs[s].at[pl.ds(k * units, units), :],
                    sems.at[s, k],
                )
            )
    for copy in copies:
        copy.start()
    for copy in copies:
        copy.wait()


def weight_pieces(g, gate, up, down, groups):
    _, units, width = gate.shape
    any_space = pl.BlockSpec(memory_space=pltpu.HBM)
    shape = jax.ShapeDtypeStruct((3 * units, width // groups), BF16)
    return pl.pallas_call(
        functools.partial(slice_kernel, groups),
        out_shape=[shape] * groups,
        in_specs=[SMEM] + [any_space] * 3,
        out_specs=[any_space] * groups,
        scratch_shapes=[pltpu.SemaphoreType.DMA((groups, 3))],
        compiler_params=pltpu.CompilerParams(vmem_limit_bytes=60 * 1024 * 1024),
        cost_estimate=cost(0, 6 * units * width * 2),
        name="weight_slices",
    )(g, gate, up, down)


def dot_nt(a, b):
    return lax.dot_general(a, b, (((1,), (1,)), ((), ())), preferred_element_type=F32)


def dot_tn(a, b):
    return lax.dot_general(a, b, (((0,), (0,)), ((), ())), preferred_element_type=F32)


def gate_up_kernel(groups, g_ref, rows_ref, *refs):
    pieces, out_ref = refs[:-1], refs[-1]
    rows = rows_ref[...].reshape(-1, rows_ref.shape[2])
    for s in range(groups):
        home = lax.rem(g_ref[0] + groups - s, groups)
        out_ref[home] = dot_nt(pieces[s][...], rows).astype(BF16)


def gate_up(g, rows, pieces):
    experts, cap, part = rows.shape
    slots = experts * cap
    groups = len(pieces)
    double = pieces[0].shape[0] * 2 // 3
    return pl.pallas_call(
        functools.partial(gate_up_kernel, groups),
        out_shape=jax.ShapeDtypeStruct((groups, double, slots), BF16),
        grid_spec=pltpu.PrefetchScalarGridSpec(
            num_scalar_prefetch=1,
            grid=(1,),
            in_specs=[pl.BlockSpec(rows.shape, lambda i, g_ref: (0, 0, 0))]
            + [pl.BlockSpec((double, part), lambda i, g_ref: (0, 0))] * groups,
            out_specs=pl.BlockSpec((groups, double, slots), lambda i, g_ref: (0, 0, 0)),
        ),
        compiler_params=PARAMS,
        cost_estimate=cost(2 * slots * part * double * groups, 6 << 20),
        name="gate_up",
    )(g, rows, *pieces)


def silu_kernel(acts_ref, out_ref):
    units = out_ref.shape[0]
    gate = jnp.sum(acts_ref[:, :units].astype(F32), axis=0)
    up = jnp.sum(acts_ref[:, units:].astype(F32), axis=0)
    out_ref[...] = (gate / (1.0 + jnp.exp(-gate)) * up).astype(BF16)


def silu(acts):
    _, double, slots = acts.shape
    return pl.pallas_call(
        silu_kernel,
        out_shape=jax.ShapeDtypeStruct((double // 2, slots), BF16),
        in_specs=[VMEM],
        out_specs=VMEM,
        compiler_params=PARAMS,
        cost_estimate=cost(8 * double * slots, 2 << 20),
        name="silu_sum",
    )(acts)


def down_kernel(groups, g_ref, hidden_ref, *refs):
    pieces, out_ref = refs[:-1], refs[-1]
    units, part = pieces[0].shape
    experts, cap, _ = out_ref.shape
    g = g_ref[0]
    chunk = part // 4
    held = [
        hidden_ref[pl.ds(pl.multiple_of(lax.rem(g + groups - s, groups) * units, units), units), :]
        for s in range(groups)
    ]
    for n in range(4):
        columns = slice(n * chunk, (n + 1) * chunk)
        total = dot_tn(held[0], pieces[0][:, columns])
        for s in range(1, groups):
            total += dot_tn(held[s], pieces[s][:, columns])
        out_ref[:, :, columns] = total.astype(BF16).reshape(experts, cap, chunk)


def down(g, hidden, pieces):
    inner, slots = hidden.shape
    groups = len(pieces)
    units, part = inner // groups, pieces[0].shape[1]
    out = (slots // CAP, CAP, part)
    return pl.pallas_call(
        functools.partial(down_kernel, groups),
        out_shape=jax.ShapeDtypeStruct(out, BF16),
        grid_spec=pltpu.PrefetchScalarGridSpec(
            num_scalar_prefetch=1,
            grid=(1,),
            in_specs=[pl.BlockSpec((inner, slots), lambda i, g_ref: (0, 0))]
            + [pl.BlockSpec((units, part), lambda i, g_ref: (2, 0))] * groups,
            out_specs=pl.BlockSpec(out, lambda i, g_ref: (0, 0, 0)),
        ),
        compiler_params=PARAMS,
        cost_estimate=cost(2 * slots * inner * part, 4 << 20),
        name="down",
    )(g, hidden, *pieces)


def combine_kernel(node_ref, table_ref, returned_ref, block_ref, known_ref, out_ref):
    dests, trees, _ = out_ref.shape
    block, part = block_ref.shape
    peers = part // 128
    groups = dests // peers
    tree = block // trees
    zs = known_ref.shape[2] // 2 // 32
    returned = returned_ref[...].reshape(-1, part)
    moe = jnp.dot(table_ref[...], returned, preferred_element_type=F32)
    result = (block_ref[...].astype(F32) + moe).astype(BF16).astype(F32)
    place = lax.broadcasted_iota(jnp.int32, (tree, part), 0)
    chosen = []
    for t in range(trees):
        rows = result[t * tree : (t + 1) * tree]
        chosen.append(jnp.sum(jnp.where(place == node_ref[t], rows, 0.0), axis=0, keepdims=True))
    chosen = jnp.concatenate(chosen, axis=0)
    for p in range(peers):
        parts = [chosen[:, z * peers * 32 + p * 32 : z * peers * 32 + p * 32 + 32] for z in range(zs)]
        high = jnp.concatenate(parts, axis=1).astype(BF16)
        lanes = slice(p * 128, p * 128 + 128)
        for j in range(groups):
            d = p * groups + j
            out_ref[d, :, 0:256] = known_ref[p]
            out_ref[d, :, 256:384] = high
            rows = result[j * tree : (j + 1) * tree, lanes]
            out_ref[d, :, 384:512] = rows[:trees].astype(BF16)
            out_ref[d, :, 512:640] = rows[trees:].astype(BF16)


def combine(nodes, table, returned, block_in, known, dests):
    block, part = block_in.shape
    trees = nodes.shape[0]
    return pl.pallas_call(
        combine_kernel,
        out_shape=jax.ShapeDtypeStruct((dests, trees, 640), BF16),
        in_specs=[SMEM] + [VMEM] * 4,
        out_specs=VMEM,
        compiler_params=PARAMS,
        cost_estimate=cost(2 * block * table.shape[1] * part, 2 << 20),
        name="combine",
    )(nodes, table, returned, block_in, known)


def join_kernel(rows_ref, tiles_ref, weight_ref, out_ref):
    amount, trees, step = tiles_ref.shape
    peers = out_ref.shape[0]
    line = 128
    quarter = weight_ref.shape[0] // trees
    high = jnp.concatenate(
        [rows_ref[:, t * step + 2 * line : t * step + 3 * line] for t in range(trees)], axis=0
    )
    row = lax.broadcasted_iota(jnp.int32, (amount, amount * trees), 0)
    column = lax.broadcasted_iota(jnp.int32, (amount, amount * trees), 1)
    place = lax.rem(column, amount)
    same = (lax.div(column, amount) == lax.rem(row, trees)) & (
        lax.div(place, trees) == lax.div(row, trees)
    )
    total = None
    for q in range(trees):
        chosen = jnp.where(same & (lax.rem(place, trees) == q), 1.0, 0.0).astype(BF16)
        parts = [
            rows_ref[:, q * step : q * step + line],
            rows_ref[:, q * step + line : q * step + 2 * line],
            jnp.dot(chosen, high, preferred_element_type=F32).astype(BF16),
        ]
        for k, values in enumerate(parts):
            weight = weight_ref[q * quarter : (q + 1) * quarter, k].reshape(line, -1)
            product = jnp.dot(values, weight, preferred_element_type=F32)
            total = product if total is None else total + product
    half = total.shape[1] // 2
    for p in range(peers):
        rows = slice(p * trees, (p + 1) * trees)
        pair = jnp.concatenate([total[rows, :half], total[rows, half:]], axis=0)
        out_ref[p, 0 : 2 * trees] = pair.astype(BF16)
        for j in range(trees):
            for h in range(2):
                lanes = slice((3 + h) * line, (4 + h) * line)
                out_ref[p, (2 + h) * trees : (3 + h) * trees, j * line : (j + 1) * line] = (
                    tiles_ref[p * trees + j, :, lanes]
                )


def join(tiles, weight):
    amount, trees, step = tiles.shape
    peers = amount // trees
    width = weight.shape[-1]
    return pl.pallas_call(
        join_kernel,
        out_shape=jax.ShapeDtypeStruct((peers, 4 * trees, width // 2), BF16),
        in_specs=[VMEM] * 3,
        out_specs=VMEM,
        compiler_params=PARAMS,
        cost_estimate=cost(2 * amount * weight.size, 4 << 20),
        name="join",
    )(tiles.reshape(amount, trees * step), tiles, weight)


def finish_kernel(back_ref, layer_ref, joined_ref):
    peers, rows, half = back_ref.shape
    trees = rows // 4
    summed = jnp.sum(back_ref[:, 0 : 2 * trees].astype(F32), axis=0)
    joined_ref[:, :half] = summed[:trees].astype(BF16)
    joined_ref[:, half:] = summed[trees:].astype(BF16)
    for p in range(peers):
        for j in range(trees):
            lane = j * 2 * half + p * 128
            layer_ref[:, lane : lane + 128] = back_ref[
                p, 2 * trees : 4 * trees, j * 128 : (j + 1) * 128
            ]


def finish(back, layer_shape, joined_shape):
    return pl.pallas_call(
        finish_kernel,
        out_shape=[
            jax.ShapeDtypeStruct(layer_shape, BF16),
            jax.ShapeDtypeStruct(joined_shape, BF16),
        ],
        in_specs=[VMEM],
        out_specs=[VMEM] * 2,
        compiler_params=PARAMS,
        cost_estimate=cost(back.size, back.size * 4),
        name="finish",
    )(back)


def route_weights(route_logits):
    exponent = jnp.exp(route_logits)
    return (exponent / jnp.sum(exponent, axis=-1, keepdims=True)).astype(BF16)


def slot_places(route_ids, experts):
    flat_ids = route_ids.reshape(-1)
    amount = flat_ids.shape[0]
    onehot = flat_ids[:, None] == jnp.arange(experts, dtype=jnp.int32)[None, :]
    lower = jnp.arange(amount)[:, None] > jnp.arange(amount)[None, :]
    before = jnp.dot(lower.astype(BF16), onehot.astype(BF16), preferred_element_type=F32)
    rank = jnp.sum(jnp.where(onehot, before, 0.0), axis=1).astype(jnp.int32)
    return flat_ids * CAP + rank


def on_device(
    layer_in,
    norm_gain,
    route_ids,
    route_logits,
    gate_proj,
    up_proj,
    down_proj,
    low_feature,
    mid_feature,
    accepted_node,
    join_weight,
):
    groups = lax.axis_size("y")
    experts = Z_SIZE * P_SIZE
    g = lax.axis_index("y").astype(jnp.int32)
    g_one = g.reshape(1)
    rows_dev, width = layer_in.shape
    block, top = route_ids.shape
    part = width // groups
    slots = experts * CAP
    trees = accepted_node.shape[0]

    join_all = lax.all_gather(join_weight, "z", axis=0, tiled=False)

    both = normed_and_raw(layer_in, norm_gain, groups)
    both = lax.all_to_all(both, "y", 0, 0, tiled=True)
    normed = both[:, 0].reshape(block, part)
    block_in = both[:, 1].reshape(block, part)

    weights = route_weights(route_logits)
    places = slot_places(route_ids, experts)
    slot_ids = jnp.arange(slots, dtype=jnp.int32)
    matches = (places[:, None] == slot_ids[None, :]).reshape(block, top, slots)
    dispatch = jnp.any(matches, axis=1).astype(BF16)
    outgoing = dot_tn(dispatch, normed).astype(BF16).reshape(experts, CAP, part)

    cut = weight_pieces(g_one, gate_proj, up_proj, down_proj, groups)
    outgoing, *cut = lax.optimization_barrier((outgoing, *cut))
    pieces = [
        lax.ppermute(piece, "y", [(j, (j + s) % groups) for j in range(groups)]) if s else piece
        for s, piece in enumerate(cut)
    ]
    received = lax.all_to_all(outgoing, EXPERT, 0, 0, tiled=True)

    combine_table = jnp.sum(
        jnp.where(matches, weights.astype(F32)[:, :, None], 0.0), axis=1
    ).astype(BF16)

    acts = gate_up(g_one, received, pieces)
    acts = lax.all_to_all(acts, "y", 0, 0, tiled=True)
    hidden = silu(acts)
    hidden_all = lax.all_gather(hidden, "y", axis=0, tiled=True)
    expert_out = down(g_one, hidden_all, pieces)
    returned = lax.all_to_all(expert_out, EXPERT, 0, 0, tiled=True)

    own_node = lax.dynamic_slice_in_dim(accepted_node, g, 1, 0)[0]
    feat = width // experts
    z_part = Z_SIZE // groups

    def known(feature):
        row = lax.dynamic_index_in_dim(feature, own_node, 0, keepdims=False)
        row = row.reshape(groups, z_part, P_SIZE, feat).transpose(2, 0, 1, 3)
        return row.reshape(P_SIZE, groups, z_part * feat)

    early = jnp.concatenate([known(low_feature), known(mid_feature)], axis=-1)
    early, combine_table, block_in, returned = lax.optimization_barrier(
        (early, combine_table, block_in, returned)
    )
    sent = combine(accepted_node, combine_table, returned, block_in, early, P_SIZE * groups)
    spread = lax.all_to_all(sent, ("p", "y"), 0, 0, tiled=True)

    back = lax.all_to_all(join(spread, join_all), "p", 0, 0, tiled=True)
    return tuple(finish(back, (rows_dev, width), (trees, part)))


def solution(mesh):
    split = Mesh(mesh.devices.reshape(Z_SIZE, P_SIZE, -1), ("z", "p", "y"))
    every = ("z", "p", "y")
    placed = (
        P(every, None),
        P(),
        P(EXPERT, None),
        P(EXPERT, None),
        P(EXPERT, "y", None),
        P(EXPERT, "y", None),
        P(EXPERT, "y", None),
        P(every, None),
        P(every, None),
        P(EXPERT),
        P(None, EXPERT, "y"),
    )
    return jax.shard_map(
        on_device,
        mesh=split,
        in_specs=placed,
        out_specs=(P(every, None), P(EXPERT, "y")),
        check_vma=False,
    )
```

```python
import functools

import jax
import jax.numpy as jnp
from jax import lax
from jax.experimental import pallas as pl
from jax.experimental.pallas import tpu as pltpu
from jax.sharding import Mesh
from jax.sharding import PartitionSpec as P

EPSILON = 1e-06
Z_SIZE = 16
P_SIZE = 8
CAP = 4
EXPERT = ("z", "p")
F32 = jnp.float32
BF16 = jnp.bfloat16
PARAMS = pltpu.CompilerParams(vmem_limit_bytes=40 * 1024 * 1024)
VMEM = pl.BlockSpec(memory_space=pltpu.VMEM)
SMEM = pl.BlockSpec(memory_space=pltpu.SMEM)


def shift_y(array, groups, shift):
    return lax.ppermute(array, "y", [(j, (j + shift) % groups) for j in range(groups)])


def cost(flops, moved):
    return pl.CostEstimate(flops=flops, bytes_accessed=moved, transcendentals=0)


def norm_kernel(layer_ref, gain_ref, out_ref):
    groups, _, _, part = out_ref.shape
    widened = layer_ref[...].astype(F32)
    inverse = lax.rsqrt(jnp.mean(widened * widened, axis=-1, keepdims=True) + EPSILON)
    gain = gain_ref[...].reshape(1, -1).astype(F32)
    normed = (widened * inverse * gain).astype(BF16)
    for j in range(groups):
        out_ref[j, 0] = normed[:, j * part : (j + 1) * part]
        out_ref[j, 1] = layer_ref[:, j * part : (j + 1) * part]


def normed_and_raw(layer_in, norm_gain, groups):
    rows, width = layer_in.shape
    return pl.pallas_call(
        norm_kernel,
        out_shape=jax.ShapeDtypeStruct((groups, 2, rows, width // groups), BF16),
        in_specs=[VMEM] * 2,
        out_specs=VMEM,
        compiler_params=PARAMS,
        cost_estimate=cost(rows * width * 6, rows * width * 6),
        name="norm_pack",
    )(layer_in, norm_gain)


def slice_kernel(shifts, groups, g_ref, *refs):
    count = len(refs) - 1 - len(shifts)
    sources, outs, sems = refs[:count], refs[count:-1], refs[-1]
    _, units, width = sources[0].shape
    part = width // groups
    copies = []
    for i, s in enumerate(shifts):
        lane = pl.multiple_of(lax.rem(g_ref[0] + s, groups) * part, part)
        for k, source in enumerate(sources):
            copies.append(
                pltpu.make_async_copy(
                    source.at[0, :, pl.ds(lane, part)],
                    outs[i].at[pl.ds(k * units, units), :],
                    sems.at[i, k],
                )
            )
    for copy in copies:
        copy.start()
    for copy in copies:
        copy.wait()


def weight_slices(g, sources, shifts, groups, name):
    _, units, width = sources[0].shape
    count = len(sources)
    shape = jax.ShapeDtypeStruct((count * units, width // groups), BF16)
    moved = 2 * len(shifts) * count * units * width // groups * 2
    return pl.pallas_call(
        functools.partial(slice_kernel, shifts, groups),
        out_shape=[shape] * len(shifts),
        in_specs=[SMEM] + [pl.BlockSpec(memory_space=pltpu.HBM)] * count,
        out_specs=[VMEM] * len(shifts),
        scratch_shapes=[pltpu.SemaphoreType.DMA((len(shifts), count))],
        compiler_params=pltpu.CompilerParams(vmem_limit_bytes=60 * 1024 * 1024),
        cost_estimate=cost(0, moved),
        name=name,
    )(g, *sources)


def dispatch_kernel(table_ref, both_ref, out_ref):
    part = both_ref.shape[3]
    normed = both_ref[:, 0].reshape(-1, part)
    rows = dot_tn(table_ref[...], normed).astype(BF16)
    out_ref[...] = rows.reshape(out_ref.shape)


def dispatch_rows(table, both):
    part = both.shape[3]
    slots = table.shape[1]
    return pl.pallas_call(
        dispatch_kernel,
        out_shape=jax.ShapeDtypeStruct((slots // CAP, CAP, part), BF16),
        in_specs=[VMEM] * 2,
        out_specs=VMEM,
        compiler_params=PARAMS,
        cost_estimate=cost(2 * table.size * part, 2 * slots * part),
        name="dispatch",
    )(table, both)


def dot_nt(a, b):
    return lax.dot_general(a, b, (((1,), (1,)), ((), ())), preferred_element_type=F32)


def dot_tn(a, b):
    return lax.dot_general(a, b, (((0,), (0,)), ((), ())), preferred_element_type=F32)


def gate_up_kernel(groups, g_ref, rows_ref, *refs):
    pieces, out_ref = refs[:-1], refs[-1]
    rows = rows_ref[...].reshape(-1, rows_ref.shape[2])
    for s in range(groups):
        home = lax.rem(g_ref[0] + groups - s, groups)
        out_ref[home] = dot_nt(pieces[s][...], rows).astype(BF16)


def gate_up(g, rows, pieces):
    experts, cap, part = rows.shape
    slots = experts * cap
    groups = len(pieces)
    double = pieces[0].shape[0]
    return pl.pallas_call(
        functools.partial(gate_up_kernel, groups),
        out_shape=jax.ShapeDtypeStruct((groups, double, slots), BF16),
        grid_spec=pltpu.PrefetchScalarGridSpec(
            num_scalar_prefetch=1,
            grid=(1,),
            in_specs=[pl.BlockSpec(rows.shape, lambda i, g_ref: (0, 0, 0))]
            + [pl.BlockSpec((double, part), lambda i, g_ref: (0, 0))] * groups,
            out_specs=pl.BlockSpec((groups, double, slots), lambda i, g_ref: (0, 0, 0)),
        ),
        compiler_params=PARAMS,
        cost_estimate=cost(2 * slots * part * double * groups, 6 << 20),
        name="gate_up",
    )(g, rows, *pieces)


def silu_kernel(acts_ref, out_ref):
    units = out_ref.shape[0]
    gate = jnp.sum(acts_ref[:, :units].astype(F32), axis=0)
    up = jnp.sum(acts_ref[:, units:].astype(F32), axis=0)
    out_ref[...] = (gate / (1.0 + jnp.exp(-gate)) * up).astype(BF16)


def silu(acts):
    _, double, slots = acts.shape
    return pl.pallas_call(
        silu_kernel,
        out_shape=jax.ShapeDtypeStruct((double // 2, slots), BF16),
        in_specs=[VMEM],
        out_specs=VMEM,
        compiler_params=PARAMS,
        cost_estimate=cost(8 * double * slots, 2 << 20),
        name="silu_sum",
    )(acts)


def down_kernel(groups, g_ref, hidden_ref, *refs):
    pieces, out_ref = refs[:-1], refs[-1]
    units, part = pieces[0].shape
    experts, cap, _ = out_ref.shape
    g = g_ref[0]
    chunk = part // 4
    held = [
        hidden_ref[pl.ds(pl.multiple_of(lax.rem(g + groups - s, groups) * units, units), units), :]
        for s in range(groups)
    ]
    for n in range(4):
        columns = slice(n * chunk, (n + 1) * chunk)
        total = dot_tn(held[0], pieces[0][:, columns])
        for s in range(1, groups):
            total += dot_tn(held[s], pieces[s][:, columns])
        out_ref[:, :, columns] = total.astype(BF16).reshape(experts, cap, chunk)


def down(g, hidden, pieces):
    inner, slots = hidden.shape
    groups = len(pieces)
    units, part = inner // groups, pieces[0].shape[1]
    out = (slots // CAP, CAP, part)
    return pl.pallas_call(
        functools.partial(down_kernel, groups),
        out_shape=jax.ShapeDtypeStruct(out, BF16),
        grid_spec=pltpu.PrefetchScalarGridSpec(
            num_scalar_prefetch=1,
            grid=(1,),
            in_specs=[pl.BlockSpec((inner, slots), lambda i, g_ref: (0, 0))]
            + [pl.BlockSpec((units, part), lambda i, g_ref: (0, 0))] * groups,
            out_specs=pl.BlockSpec(out, lambda i, g_ref: (0, 0, 0)),
        ),
        compiler_params=PARAMS,
        cost_estimate=cost(2 * slots * inner * part, 4 << 20),
        name="down",
    )(g, hidden, *pieces)


def combine_kernel(node_ref, table_ref, returned_ref, block_ref, known_ref, out_ref):
    dests, trees, _ = out_ref.shape
    block, part = block_ref.shape
    peers = part // 128
    groups = dests // peers
    tree = block // trees
    zs = known_ref.shape[2] // 2 // 32
    returned = returned_ref[...].reshape(-1, part)
    moe = jnp.dot(table_ref[...], returned, preferred_element_type=F32)
    result = (block_ref[...].astype(F32) + moe).astype(BF16).astype(F32)
    place = lax.broadcasted_iota(jnp.int32, (tree, part), 0)
    chosen = []
    for t in range(trees):
        rows = result[t * tree : (t + 1) * tree]
        chosen.append(jnp.sum(jnp.where(place == node_ref[t], rows, 0.0), axis=0, keepdims=True))
    chosen = jnp.concatenate(chosen, axis=0)
    for p in range(peers):
        parts = [chosen[:, z * peers * 32 + p * 32 : z * peers * 32 + p * 32 + 32] for z in range(zs)]
        high = jnp.concatenate(parts, axis=1).astype(BF16)
        lanes = slice(p * 128, p * 128 + 128)
        for j in range(groups):
            d = p * groups + j
            out_ref[d, :, 0:256] = known_ref[p]
            out_ref[d, :, 256:384] = high
            rows = result[j * tree : (j + 1) * tree, lanes]
            out_ref[d, :, 384:512] = rows[:trees].astype(BF16)
            out_ref[d, :, 512:640] = rows[trees:].astype(BF16)


def combine(nodes, table, returned, block_in, known, dests):
    block, part = block_in.shape
    trees = nodes.shape[0]
    return pl.pallas_call(
        combine_kernel,
        out_shape=jax.ShapeDtypeStruct((dests, trees, 640), BF16),
        in_specs=[SMEM] + [VMEM] * 4,
        out_specs=VMEM,
        compiler_params=PARAMS,
        cost_estimate=cost(2 * block * table.shape[1] * part, 2 << 20),
        name="combine",
    )(nodes, table, returned, block_in, known)


def join_kernel(rows_ref, tiles_ref, weight_ref, out_ref):
    amount, trees, step = tiles_ref.shape
    peers = out_ref.shape[0]
    line = 128
    quarter = weight_ref.shape[0] // trees
    high = jnp.concatenate(
        [rows_ref[:, t * step + 2 * line : t * step + 3 * line] for t in range(trees)], axis=0
    )
    row = lax.broadcasted_iota(jnp.int32, (amount, amount * trees), 0)
    column = lax.broadcasted_iota(jnp.int32, (amount, amount * trees), 1)
    place = lax.rem(column, amount)
    same = (lax.div(column, amount) == lax.rem(row, trees)) & (
        lax.div(place, trees) == lax.div(row, trees)
    )
    total = None
    for q in range(trees):
        chosen = jnp.where(same & (lax.rem(place, trees) == q), 1.0, 0.0).astype(BF16)
        parts = [
            rows_ref[:, q * step : q * step + line],
            rows_ref[:, q * step + line : q * step + 2 * line],
            jnp.dot(chosen, high, preferred_element_type=F32).astype(BF16),
        ]
        for k, values in enumerate(parts):
            weight = weight_ref[q * quarter : (q + 1) * quarter, k].reshape(line, -1)
            product = jnp.dot(values, weight, preferred_element_type=F32)
            total = product if total is None else total + product
    half = total.shape[1] // 2
    for p in range(peers):
        rows = slice(p * trees, (p + 1) * trees)
        pair = jnp.concatenate([total[rows, :half], total[rows, half:]], axis=0)
        out_ref[p, 0 : 2 * trees] = pair.astype(BF16)
        for j in range(trees):
            for h in range(2):
                lanes = slice((3 + h) * line, (4 + h) * line)
                out_ref[p, (2 + h) * trees : (3 + h) * trees, j * line : (j + 1) * line] = (
                    tiles_ref[p * trees + j, :, lanes]
                )


def join(tiles, weight):
    amount, trees, step = tiles.shape
    peers = amount // trees
    width = weight.shape[-1]
    return pl.pallas_call(
        join_kernel,
        out_shape=jax.ShapeDtypeStruct((peers, 4 * trees, width // 2), BF16),
        in_specs=[VMEM] * 3,
        out_specs=VMEM,
        compiler_params=PARAMS,
        cost_estimate=cost(2 * amount * weight.size, 4 << 20),
        name="join",
    )(tiles.reshape(amount, trees * step), tiles, weight)


def finish_kernel(back_ref, layer_ref, joined_ref):
    peers, rows, half = back_ref.shape
    trees = rows // 4
    summed = jnp.sum(back_ref[:, 0 : 2 * trees].astype(F32), axis=0)
    joined_ref[:, :half] = summed[:trees].astype(BF16)
    joined_ref[:, half:] = summed[trees:].astype(BF16)
    for p in range(peers):
        for j in range(trees):
            lane = j * 2 * half + p * 128
            layer_ref[:, lane : lane + 128] = back_ref[
                p, 2 * trees : 4 * trees, j * 128 : (j + 1) * 128
            ]


def finish(back, layer_shape, joined_shape):
    return pl.pallas_call(
        finish_kernel,
        out_shape=[
            jax.ShapeDtypeStruct(layer_shape, BF16),
            jax.ShapeDtypeStruct(joined_shape, BF16),
        ],
        in_specs=[VMEM],
        out_specs=[VMEM] * 2,
        compiler_params=PARAMS,
        cost_estimate=cost(back.size, back.size * 4),
        name="finish",
    )(back)


def route_weights(route_logits):
    exponent = jnp.exp(route_logits)
    return (exponent / jnp.sum(exponent, axis=-1, keepdims=True)).astype(BF16)


def slot_places(route_ids, experts):
    flat_ids = route_ids.reshape(-1)
    amount = flat_ids.shape[0]
    onehot = flat_ids[:, None] == jnp.arange(experts, dtype=jnp.int32)[None, :]
    lower = jnp.arange(amount)[:, None] > jnp.arange(amount)[None, :]
    before = jnp.dot(lower.astype(BF16), onehot.astype(BF16), preferred_element_type=F32)
    rank = jnp.sum(jnp.where(onehot, before, 0.0), axis=1).astype(jnp.int32)
    return flat_ids * CAP + rank


def on_device(
    layer_in,
    norm_gain,
    route_ids,
    route_logits,
    gate_proj,
    up_proj,
    down_proj,
    low_feature,
    mid_feature,
    accepted_node,
    join_weight,
):
    groups = lax.axis_size("y")
    experts = Z_SIZE * P_SIZE
    g = lax.axis_index("y").astype(jnp.int32)
    g_one = g.reshape(1)
    rows_dev, width = layer_in.shape
    block, top = route_ids.shape
    part = width // groups
    slots = experts * CAP
    trees = accepted_node.shape[0]

    join_all = lax.all_gather(join_weight, "z", axis=0, tiled=False)

    both = normed_and_raw(layer_in, norm_gain, groups)
    both = lax.all_to_all(both, "y", 0, 0, tiled=True)
    block_in = both[:, 1].reshape(block, part)

    weights = route_weights(route_logits)
    places = slot_places(route_ids, experts)
    slot_ids = jnp.arange(slots, dtype=jnp.int32)
    matches = (places[:, None] == slot_ids[None, :]).reshape(block, top, slots)
    dispatch = jnp.any(matches, axis=1).astype(BF16)
    outgoing = dispatch_rows(dispatch, both)

    others = tuple(range(1, groups))
    both_in = [gate_proj, up_proj]
    cut = weight_slices(g_one, both_in, others, groups, "gate_up_slices")
    outgoing, *cut = lax.optimization_barrier((outgoing, *cut))
    gate_up_pieces = [shift_y(piece, groups, s) for s, piece in zip(others, cut)]
    cut = weight_slices(g_one, [down_proj], others, groups, "down_slices")
    down_pieces = [shift_y(piece, groups, s) for s, piece in zip(others, cut)]
    gate_up_pieces = [*weight_slices(g_one, both_in, (0,), groups, "gate_up_own"), *gate_up_pieces]
    down_pieces = [*weight_slices(g_one, [down_proj], (0,), groups, "down_own"), *down_pieces]
    received = lax.all_to_all(outgoing, EXPERT, 0, 0, tiled=True)

    combine_table = jnp.sum(
        jnp.where(matches, weights.astype(F32)[:, :, None], 0.0), axis=1
    ).astype(BF16)

    acts = gate_up(g_one, received, gate_up_pieces)
    acts, *down_pieces = lax.optimization_barrier((acts, *down_pieces))
    acts = lax.all_to_all(acts, "y", 0, 0, tiled=True)
    hidden = silu(acts)
    hidden_all = lax.all_gather(hidden, "y", axis=0, tiled=True)
    expert_out = down(g_one, hidden_all, down_pieces)
    returned = lax.all_to_all(expert_out, EXPERT, 0, 0, tiled=True)

    own_node = lax.dynamic_slice_in_dim(accepted_node, g, 1, 0)[0]
    feat = width // experts
    z_part = Z_SIZE // groups

    def known(feature):
        row = lax.dynamic_index_in_dim(feature, own_node, 0, keepdims=False)
        row = row.reshape(groups, z_part, P_SIZE, feat).transpose(2, 0, 1, 3)
        return row.reshape(P_SIZE, groups, z_part * feat)

    early = jnp.concatenate([known(low_feature), known(mid_feature)], axis=-1)
    early, combine_table, block_in, join_all, returned = lax.optimization_barrier(
        (early, combine_table, block_in, join_all, returned)
    )
    sent = combine(accepted_node, combine_table, returned, block_in, early, P_SIZE * groups)
    spread = lax.all_to_all(sent, ("p", "y"), 0, 0, tiled=True)

    back = lax.all_to_all(join(spread, join_all), "p", 0, 0, tiled=True)
    return tuple(finish(back, (rows_dev, width), (trees, part)))


def solution(mesh):
    split = Mesh(mesh.devices.reshape(Z_SIZE, P_SIZE, -1), ("z", "p", "y"))
    every = ("z", "p", "y")
    placed = (
        P(every, None),
        P(),
        P(EXPERT, None),
        P(EXPERT, None),
        P(EXPERT, "y", None),
        P(EXPERT, "y", None),
        P(EXPERT, "y", None),
        P(every, None),
        P(every, None),
        P(EXPERT),
        P(None, EXPERT, "y"),
    )
    return jax.shard_map(
        on_device,
        mesh=split,
        in_specs=placed,
        out_specs=(P(every, None), P(EXPERT, "y")),
        check_vma=False,
    )
```

```python
import functools

import jax
import jax.numpy as jnp
from jax import lax
from jax.experimental import pallas as pl
from jax.experimental.pallas import tpu as pltpu
from jax.sharding import Mesh
from jax.sharding import PartitionSpec as P

EPSILON = 1e-06
Z_SIZE = 16
P_SIZE = 8
CAP = 4
EXPERT = ("z", "p")
LINE = 128
F32 = jnp.float32
BF16 = jnp.bfloat16
PARAMS = pltpu.CompilerParams(vmem_limit_bytes=40 * 1024 * 1024)
VMEM = pl.BlockSpec(memory_space=pltpu.VMEM)
SMEM = pl.BlockSpec(memory_space=pltpu.SMEM)


def shift_y(array, groups, shift):
    return lax.ppermute(array, "y", [(j, (j + shift) % groups) for j in range(groups)])


def cost(flops, moved):
    return pl.CostEstimate(flops=flops, bytes_accessed=moved, transcendentals=0)


def prepare_kernel(g_ref, layer_ref, gain_ref, ids_ref, logits_ref, out_ref, table_ref):
    dests, rows, step = out_ref.shape
    part = step - 2 * LINE
    groups = layer_ref.shape[1] // part
    top, block = ids_ref.shape
    widened = layer_ref[...].astype(F32)
    inverse = lax.rsqrt(jnp.mean(widened * widened, axis=-1, keepdims=True) + EPSILON)
    gain = gain_ref[...].reshape(1, -1).astype(F32)
    normed = (widened * inverse * gain).astype(BF16)

    exponent = jnp.exp(logits_ref[...])
    share = exponent / jnp.sum(exponent, axis=0, keepdims=True)
    expert = lax.broadcasted_iota(jnp.int32, (LINE, block), 0)
    named = jnp.zeros((LINE, block), F32)
    weight = jnp.zeros((LINE, block), F32)
    for k in range(top):
        same = expert == ids_ref[k : k + 1, :]
        named = jnp.where(same, 1.0, named)
        weight = jnp.where(same, share[k : k + 1, :], weight)
    first = lax.broadcasted_iota(jnp.int32, (block, block), 0)
    second = lax.broadcasted_iota(jnp.int32, (block, block), 1)
    earlier = jnp.where(first < second, 1.0, 0.0).astype(BF16)
    before = jnp.dot(named.astype(BF16), earlier, preferred_element_type=F32)
    ranked = jnp.where(named > 0.0, before + 1.0, 0.0).astype(BF16)
    square = (LINE, LINE)
    unit = lax.broadcasted_iota(jnp.int32, square, 0) == lax.broadcasted_iota(jnp.int32, square, 1)
    unit = jnp.where(unit, 1.0, 0.0).astype(BF16)
    table_ref[:, :LINE] = dot_tn(ranked, unit)
    table_ref[:, LINE:] = dot_tn(weight.astype(BF16), unit)
    own = table_ref[pl.ds(pl.multiple_of(g_ref[0] * rows, rows), rows), :].astype(BF16)
    for d in range(dests):
        j = d % groups
        out_ref[d, :, :part] = normed[:, j * part : (j + 1) * part]
        out_ref[d, :, part:] = own


def prepare(g, layer_in, norm_gain, ids, logits, groups):
    rows, width = layer_in.shape
    shape = (P_SIZE * groups, rows, width // groups + 2 * LINE)
    return pl.pallas_call(
        prepare_kernel,
        out_shape=jax.ShapeDtypeStruct(shape, BF16),
        in_specs=[SMEM] + [VMEM] * 4,
        out_specs=VMEM,
        scratch_shapes=[pltpu.VMEM((ids.shape[1], 2 * LINE), F32)],
        compiler_params=PARAMS,
        cost_estimate=cost(rows * width * 6, 2 << 20),
        name="prepare",
    )(g, layer_in, norm_gain, ids, logits)


def slice_kernel(shifts, groups, g_ref, *refs):
    count = len(refs) - 1 - len(shifts)
    sources, outs, sems = refs[:count], refs[count:-1], refs[-1]
    _, units, width = sources[0].shape
    part = width // groups
    copies = []
    for i, s in enumerate(shifts):
        lane = pl.multiple_of(lax.rem(g_ref[0] + s, groups) * part, part)
        for k, source in enumerate(sources):
            copies.append(
                pltpu.make_async_copy(
                    source.at[0, :, pl.ds(lane, part)],
                    outs[i].at[pl.ds(k * units, units), :],
                    sems.at[i, k],
                )
            )
    for copy in copies:
        copy.start()
    for copy in copies:
        copy.wait()


def weight_slices(g, sources, shifts, groups, name):
    _, units, width = sources[0].shape
    count = len(sources)
    shape = jax.ShapeDtypeStruct((count * units, width // groups), BF16)
    moved = 2 * len(shifts) * count * units * width // groups * 2
    return pl.pallas_call(
        functools.partial(slice_kernel, shifts, groups),
        out_shape=[shape] * len(shifts),
        in_specs=[SMEM] + [pl.BlockSpec(memory_space=pltpu.HBM)] * count,
        out_specs=[VMEM] * len(shifts),
        scratch_shapes=[pltpu.SemaphoreType.DMA((len(shifts), count))],
        compiler_params=pltpu.CompilerParams(vmem_limit_bytes=60 * 1024 * 1024),
        cost_estimate=cost(0, moved),
        name=name,
    )(g, *sources)


def dispatch_kernel(p_ref, tokens_ref, out_ref, combine_ref):
    z_size, per_z, part = out_ref.shape
    amount, slots = combine_ref.shape
    tokens = tokens_ref[...].reshape(amount, -1)
    block = amount // P_SIZE
    expert = lax.broadcasted_iota(jnp.int32, (LINE, slots), 0)
    column = lax.broadcasted_iota(jnp.int32, (LINE, slots), 1)
    chosen = expert == lax.div(column, per_z) * P_SIZE + p_ref[0]
    chosen = jnp.where(chosen, 1.0, 0.0).astype(BF16)
    rank = jnp.dot(tokens[:, part : part + LINE], chosen, preferred_element_type=F32)
    weight = jnp.dot(tokens[:, part + LINE :], chosen, preferred_element_type=F32)
    token = lax.broadcasted_iota(jnp.int32, (amount, slots), 0)
    column = lax.broadcasted_iota(jnp.int32, (amount, slots), 1)
    wanted = lax.rem(column, CAP) + 1
    match = (rank == wanted.astype(F32)) & (
        lax.div(token, block) == lax.rem(lax.div(column, CAP), P_SIZE)
    )
    combine_ref[...] = jnp.where(match, weight, 0.0).astype(BF16)
    onehot = jnp.where(match, 1.0, 0.0).astype(BF16)
    out_ref[...] = dot_tn(onehot, tokens[:, :part]).astype(BF16).reshape(out_ref.shape)


def dispatch_rows(p, tokens):
    sources, rows, step = tokens.shape
    part = step - 2 * LINE
    per_z = P_SIZE * CAP
    slots = Z_SIZE * per_z
    return pl.pallas_call(
        dispatch_kernel,
        out_shape=[
            jax.ShapeDtypeStruct((Z_SIZE, per_z, part), BF16),
            jax.ShapeDtypeStruct((sources * rows, slots), BF16),
        ],
        in_specs=[SMEM, VMEM],
        out_specs=[VMEM] * 2,
        compiler_params=PARAMS,
        cost_estimate=cost(2 * slots * sources * rows * part, 2 * slots * part),
        name="dispatch",
    )(p, tokens)


def dot_nt(a, b):
    return lax.dot_general(a, b, (((1,), (1,)), ((), ())), preferred_element_type=F32)


def dot_tn(a, b):
    return lax.dot_general(a, b, (((0,), (0,)), ((), ())), preferred_element_type=F32)


def gate_up_kernel(groups, g_ref, rows_ref, *refs):
    pieces, out_ref = refs[:-1], refs[-1]
    rows = rows_ref[...].reshape(-1, rows_ref.shape[2])
    for s in range(groups):
        home = lax.rem(g_ref[0] + groups - s, groups)
        out_ref[home] = dot_nt(pieces[s][...], rows).astype(BF16)


def gate_up(g, rows, pieces):
    z_size, per_z, part = rows.shape
    slots = z_size * per_z
    groups = len(pieces)
    double = pieces[0].shape[0]
    return pl.pallas_call(
        functools.partial(gate_up_kernel, groups),
        out_shape=jax.ShapeDtypeStruct((groups, double, slots), BF16),
        grid_spec=pltpu.PrefetchScalarGridSpec(
            num_scalar_prefetch=1,
            grid=(1,),
            in_specs=[pl.BlockSpec(rows.shape, lambda i, g_ref: (0, 0, 0))]
            + [pl.BlockSpec((double, part), lambda i, g_ref: (0, 0))] * groups,
            out_specs=pl.BlockSpec((groups, double, slots), lambda i, g_ref: (0, 0, 0)),
        ),
        compiler_params=PARAMS,
        cost_estimate=cost(2 * slots * part * double * groups, 6 << 20),
        name="gate_up",
    )(g, rows, *pieces)


def silu_kernel(acts_ref, out_ref):
    units = out_ref.shape[0]
    gate = jnp.sum(acts_ref[:, :units].astype(F32), axis=0)
    up = jnp.sum(acts_ref[:, units:].astype(F32), axis=0)
    out_ref[...] = (gate / (1.0 + jnp.exp(-gate)) * up).astype(BF16)


def silu(acts):
    _, double, slots = acts.shape
    return pl.pallas_call(
        silu_kernel,
        out_shape=jax.ShapeDtypeStruct((double // 2, slots), BF16),
        in_specs=[VMEM],
        out_specs=VMEM,
        compiler_params=PARAMS,
        cost_estimate=cost(8 * double * slots, 2 << 20),
        name="silu_sum",
    )(acts)


def down_kernel(groups, g_ref, hidden_ref, *refs):
    pieces, out_ref = refs[:-1], refs[-1]
    units, part = pieces[0].shape
    z_size, per_z, _ = out_ref.shape
    g = g_ref[0]
    chunk = part // 4
    held = [
        hidden_ref[pl.ds(pl.multiple_of(lax.rem(g + groups - s, groups) * units, units), units), :]
        for s in range(groups)
    ]
    for n in range(4):
        columns = slice(n * chunk, (n + 1) * chunk)
        total = dot_tn(held[0], pieces[0][:, columns])
        for s in range(1, groups):
            total += dot_tn(held[s], pieces[s][:, columns])
        out_ref[:, :, columns] = total.astype(BF16).reshape(z_size, per_z, chunk)


def down(g, hidden, pieces):
    inner, slots = hidden.shape
    groups = len(pieces)
    units, part = inner // groups, pieces[0].shape[1]
    out = (Z_SIZE, slots // Z_SIZE, part)
    return pl.pallas_call(
        functools.partial(down_kernel, groups),
        out_shape=jax.ShapeDtypeStruct(out, BF16),
        grid_spec=pltpu.PrefetchScalarGridSpec(
            num_scalar_prefetch=1,
            grid=(1,),
            in_specs=[pl.BlockSpec((inner, slots), lambda i, g_ref: (0, 0))]
            + [pl.BlockSpec((units, part), lambda i, g_ref: (0, 0))] * groups,
            out_specs=pl.BlockSpec(out, lambda i, g_ref: (0, 0, 0)),
        ),
        compiler_params=PARAMS,
        cost_estimate=cost(2 * slots * inner * part, 4 << 20),
        name="down",
    )(g, hidden, *pieces)


def column_kernel(table_ref, returned_ref, out_ref):
    returned = returned_ref[...].reshape(-1, out_ref.shape[2])
    moe = jnp.dot(table_ref[...], returned, preferred_element_type=F32)
    out_ref[...] = moe.astype(BF16).reshape(out_ref.shape)


def column_sum(table, returned):
    amount, slots = table.shape
    part = returned.shape[2]
    return pl.pallas_call(
        column_kernel,
        out_shape=jax.ShapeDtypeStruct((P_SIZE, amount // P_SIZE, part), BF16),
        in_specs=[VMEM] * 2,
        out_specs=VMEM,
        compiler_params=PARAMS,
        cost_estimate=cost(2 * amount * slots * part, 2 << 20),
        name="column_sum",
    )(table, returned)


def combine_kernel(node_ref, parts_ref, known_ref, out_ref):
    dests, trees, _ = out_ref.shape
    _, block, part = parts_ref.shape
    groups = dests // P_SIZE
    tree = block // trees
    zs = LINE // 32
    result = jnp.sum(parts_ref[...].astype(F32), axis=0)
    place = lax.broadcasted_iota(jnp.int32, (tree, part), 0)
    chosen = []
    for t in range(trees):
        rows = result[t * tree : (t + 1) * tree]
        chosen.append(jnp.sum(jnp.where(place == node_ref[t], rows, 0.0), axis=0, keepdims=True))
    chosen = jnp.concatenate(chosen, axis=0)
    for p in range(P_SIZE):
        first = [(z * P_SIZE + p) * 32 for z in range(zs)]
        high = jnp.concatenate([chosen[:, f : f + 32] for f in first], axis=1).astype(BF16)
        lanes = slice(p * LINE, (p + 1) * LINE)
        for j in range(groups):
            d = p * groups + j
            out_ref[d, :, : 3 * LINE] = known_ref[p]
            out_ref[d, :, 3 * LINE : 4 * LINE] = high
            rows = result[j * tree : (j + 1) * tree, lanes]
            out_ref[d, :, 4 * LINE : 5 * LINE] = rows[:trees].astype(BF16)
            out_ref[d, :, 5 * LINE :] = rows[trees:].astype(BF16)


def combine(nodes, parts, known, dests):
    trees = nodes.shape[0]
    return pl.pallas_call(
        combine_kernel,
        out_shape=jax.ShapeDtypeStruct((dests, trees, 6 * LINE), BF16),
        in_specs=[SMEM] + [VMEM] * 2,
        out_specs=VMEM,
        compiler_params=PARAMS,
        cost_estimate=cost(parts.size * 2, 1 << 20),
        name="combine",
    )(nodes, parts, known)


def join_kernel(rows_ref, tiles_ref, weight_ref, out_ref):
    amount, trees, step = tiles_ref.shape
    quarter = weight_ref.shape[0] // trees

    def lanes_of(t, k):
        return slice(t * step + k * LINE, t * step + (k + 1) * LINE)

    high = jnp.concatenate([rows_ref[:, lanes_of(t, 3)] for t in range(trees)], axis=0)
    row = lax.broadcasted_iota(jnp.int32, (amount, amount * trees), 0)
    column = lax.broadcasted_iota(jnp.int32, (amount, amount * trees), 1)
    place = lax.rem(column, amount)
    same = (lax.div(column, amount) == lax.rem(row, trees)) & (
        lax.div(place, trees) == lax.div(row, trees)
    )
    total = None
    for q in range(trees):
        chosen = jnp.where(same & (lax.rem(place, trees) == q), 1.0, 0.0).astype(BF16)
        moe = jnp.dot(chosen, high, preferred_element_type=F32)
        parts = [
            rows_ref[:, lanes_of(q, 0)],
            rows_ref[:, lanes_of(q, 1)],
            (rows_ref[:, lanes_of(q, 2)].astype(F32) + moe).astype(BF16),
        ]
        for k, values in enumerate(parts):
            weight = weight_ref[q * quarter : (q + 1) * quarter, k].reshape(LINE, -1)
            product = jnp.dot(values, weight, preferred_element_type=F32)
            total = product if total is None else total + product
    half = total.shape[1] // 2
    for p in range(P_SIZE):
        rows = slice(p * trees, (p + 1) * trees)
        pair = jnp.concatenate([total[rows, :half], total[rows, half:]], axis=0)
        out_ref[p, 0 : 2 * trees] = pair.astype(BF16)
        for j in range(trees):
            for h in range(2):
                out_ref[p, (2 + h) * trees : (3 + h) * trees, j * LINE : (j + 1) * LINE] = (
                    tiles_ref[p * trees + j, :, (4 + h) * LINE : (5 + h) * LINE]
                )


def join(tiles, weight):
    amount, trees, step = tiles.shape
    peers = amount // trees
    width = weight.shape[-1]
    return pl.pallas_call(
        join_kernel,
        out_shape=jax.ShapeDtypeStruct((peers, 4 * trees, width // 2), BF16),
        in_specs=[VMEM] * 3,
        out_specs=VMEM,
        compiler_params=PARAMS,
        cost_estimate=cost(2 * amount * weight.size, 4 << 20),
        name="join",
    )(tiles.reshape(amount, trees * step), tiles, weight)


def finish_kernel(back_ref, layer_in_ref, layer_ref, joined_ref):
    peers, rows, half = back_ref.shape
    trees = rows // 4
    summed = jnp.sum(back_ref[:, 0 : 2 * trees].astype(F32), axis=0)
    joined_ref[:, :half] = summed[:trees].astype(BF16)
    joined_ref[:, half:] = summed[trees:].astype(BF16)
    for p in range(peers):
        for j in range(trees):
            lane = j * 2 * half + p * LINE
            moe = back_ref[p, 2 * trees : 4 * trees, j * LINE : (j + 1) * LINE].astype(F32)
            own = layer_in_ref[:, lane : lane + LINE].astype(F32)
            layer_ref[:, lane : lane + LINE] = (own + moe).astype(BF16)


def finish(back, layer_in, joined_shape):
    return pl.pallas_call(
        finish_kernel,
        out_shape=[
            jax.ShapeDtypeStruct(layer_in.shape, BF16),
            jax.ShapeDtypeStruct(joined_shape, BF16),
        ],
        in_specs=[VMEM] * 2,
        out_specs=[VMEM] * 2,
        compiler_params=PARAMS,
        cost_estimate=cost(back.size, back.size * 4),
        name="finish",
    )(back, layer_in)


def on_device(
    layer_in,
    norm_gain,
    route_ids,
    route_logits,
    gate_proj,
    up_proj,
    down_proj,
    low_feature,
    mid_feature,
    accepted_node,
    join_weight,
):
    groups = lax.axis_size("y")
    g = lax.axis_index("y").astype(jnp.int32)
    g_one = g.reshape(1)
    p_one = lax.axis_index("p").astype(jnp.int32).reshape(1)
    width = layer_in.shape[1]
    part = width // groups
    trees = accepted_node.shape[0]

    join_all = lax.all_gather(join_weight, "z", axis=0, tiled=False)

    tokens = prepare(g_one, layer_in, norm_gain, route_ids.T, route_logits.T, groups)
    tokens = lax.all_to_all(tokens, ("p", "y"), 0, 0, tiled=True)
    outgoing, table = dispatch_rows(p_one, tokens)

    others = tuple(range(1, groups))
    both_in = [gate_proj, up_proj]
    cut = weight_slices(g_one, both_in, others, groups, "gate_up_slices")
    outgoing, *cut = lax.optimization_barrier((outgoing, *cut))
    gate_up_pieces = [shift_y(piece, groups, s) for s, piece in zip(others, cut)]
    cut = weight_slices(g_one, [down_proj], others, groups, "down_slices")
    down_pieces = [shift_y(piece, groups, s) for s, piece in zip(others, cut)]
    gate_up_pieces = [*weight_slices(g_one, both_in, (0,), groups, "gate_up_own"), *gate_up_pieces]
    down_pieces = [*weight_slices(g_one, [down_proj], (0,), groups, "down_own"), *down_pieces]
    received = lax.all_to_all(outgoing, "z", 0, 0, tiled=True)

    acts = gate_up(g_one, received, gate_up_pieces)
    acts, *down_pieces = lax.optimization_barrier((acts, *down_pieces))
    acts = lax.all_to_all(acts, "y", 0, 0, tiled=True)
    hidden = silu(acts)
    hidden_all = lax.all_gather(hidden, "y", axis=0, tiled=True)
    expert_out = down(g_one, hidden_all, down_pieces)
    returned = lax.all_to_all(expert_out, "z", 0, 0, tiled=True)

    own_node = lax.dynamic_slice_in_dim(accepted_node, g, 1, 0)[0]
    feat = width // (Z_SIZE * P_SIZE)
    z_part = Z_SIZE // groups

    def known(feature):
        row = lax.dynamic_index_in_dim(feature, own_node, 0, keepdims=False)
        row = row.reshape(groups, z_part, P_SIZE, feat).transpose(2, 0, 1, 3)
        return row.reshape(P_SIZE, groups, z_part * feat)

    early = jnp.concatenate([known(f) for f in (low_feature, mid_feature, layer_in)], axis=-1)
    early, table, join_all, returned = lax.optimization_barrier((early, table, join_all, returned))
    parts = lax.all_to_all(column_sum(table, returned), "p", 0, 0, tiled=True)

    sent = combine(accepted_node, parts, early, P_SIZE * groups)
    spread = lax.all_to_all(sent, ("p", "y"), 0, 0, tiled=True)

    back = lax.all_to_all(join(spread, join_all), "p", 0, 0, tiled=True)
    return tuple(finish(back, layer_in, (trees, part)))


def solution(mesh):
    split = Mesh(mesh.devices.reshape(Z_SIZE, P_SIZE, -1), ("z", "p", "y"))
    every = ("z", "p", "y")
    placed = (
        P(every, None),
        P(),
        P(EXPERT, None),
        P(EXPERT, None),
        P(EXPERT, "y", None),
        P(EXPERT, "y", None),
        P(EXPERT, "y", None),
        P(every, None),
        P(every, None),
        P(EXPERT),
        P(None, EXPERT, "y"),
    )
    return jax.shard_map(
        on_device,
        mesh=split,
        in_specs=placed,
        out_specs=(P(every, None), P(EXPERT, "y")),
        check_vma=False,
    )
```

```python
import functools

import jax
import jax.numpy as jnp
from jax import lax
from jax.experimental import pallas as pl
from jax.experimental.pallas import tpu as pltpu
from jax.sharding import Mesh
from jax.sharding import PartitionSpec as P

EPSILON = 1e-06
Z_SIZE = 16
P_SIZE = 8
CAP = 4
LINE = 128
EXPERT = ("zh", "zl", "p")
NEAR = ("zl", "p")
NEAR_SIZE = 2 * P_SIZE
F32 = jnp.float32
BF16 = jnp.bfloat16
PARAMS = pltpu.CompilerParams(vmem_limit_bytes=40 * 1024 * 1024)
VMEM = pl.BlockSpec(memory_space=pltpu.VMEM)
SMEM = pl.BlockSpec(memory_space=pltpu.SMEM)


def shift_y(array, groups, shift):
    return lax.ppermute(array, "y", [(j, (j + shift) % groups) for j in range(groups)])


def cost(flops, moved):
    return pl.CostEstimate(flops=flops, bytes_accessed=moved, transcendentals=0)


def norm_kernel(layer_ref, gain_ref, out_ref):
    groups, _, _, part = out_ref.shape
    widened = layer_ref[...].astype(F32)
    inverse = lax.rsqrt(jnp.mean(widened * widened, axis=-1, keepdims=True) + EPSILON)
    gain = gain_ref[...].reshape(1, -1).astype(F32)
    normed = (widened * inverse * gain).astype(BF16)
    for j in range(groups):
        out_ref[j, 0] = normed[:, j * part : (j + 1) * part]
        out_ref[j, 1] = layer_ref[:, j * part : (j + 1) * part]


def normed_and_raw(layer_in, norm_gain, groups):
    rows, width = layer_in.shape
    return pl.pallas_call(
        norm_kernel,
        out_shape=jax.ShapeDtypeStruct((groups, 2, rows, width // groups), BF16),
        in_specs=[VMEM] * 2,
        out_specs=VMEM,
        compiler_params=PARAMS,
        cost_estimate=cost(rows * width * 6, rows * width * 6),
        name="norm_pack",
    )(layer_in, norm_gain)


def slice_kernel(shifts, groups, g_ref, *refs):
    count = len(refs) - 1 - len(shifts)
    sources, outs, sems = refs[:count], refs[count:-1], refs[-1]
    _, units, width = sources[0].shape
    part = width // groups
    copies = []
    for i, s in enumerate(shifts):
        lane = pl.multiple_of(lax.rem(g_ref[0] + s, groups) * part, part)
        for k, source in enumerate(sources):
            copies.append(
                pltpu.make_async_copy(
                    source.at[0, :, pl.ds(lane, part)],
                    outs[i].at[pl.ds(k * units, units), :],
                    sems.at[i, k],
                )
            )
    for copy in copies:
        copy.start()
    for copy in copies:
        copy.wait()


def weight_slices(g, sources, shifts, groups, name):
    _, units, width = sources[0].shape
    count = len(sources)
    shape = jax.ShapeDtypeStruct((count * units, width // groups), BF16)
    moved = 2 * len(shifts) * count * units * width // groups * 2
    return pl.pallas_call(
        functools.partial(slice_kernel, shifts, groups),
        out_shape=[shape] * len(shifts),
        in_specs=[SMEM] + [pl.BlockSpec(memory_space=pltpu.HBM)] * count,
        out_specs=[VMEM] * len(shifts),
        scratch_shapes=[pltpu.SemaphoreType.DMA((len(shifts), count))],
        compiler_params=pltpu.CompilerParams(vmem_limit_bytes=60 * 1024 * 1024),
        cost_estimate=cost(0, moved),
        name=name,
    )(g, *sources)


def dispatch_kernel(table_ref, both_ref, out_ref):
    part = both_ref.shape[3]
    normed = both_ref[:, 0].reshape(-1, part)
    rows = dot_tn(table_ref[...], normed).astype(BF16)
    out_ref[...] = rows.reshape(out_ref.shape)


def dispatch_rows(table, both):
    part = both.shape[3]
    slots = table.shape[1]
    return pl.pallas_call(
        dispatch_kernel,
        out_shape=jax.ShapeDtypeStruct((slots // CAP, CAP, part), BF16),
        in_specs=[VMEM] * 2,
        out_specs=VMEM,
        compiler_params=PARAMS,
        cost_estimate=cost(2 * table.size * part, 2 * slots * part),
        name="dispatch",
    )(table, both)


def dot_nt(a, b):
    return lax.dot_general(a, b, (((1,), (1,)), ((), ())), preferred_element_type=F32)


def dot_tn(a, b):
    return lax.dot_general(a, b, (((0,), (0,)), ((), ())), preferred_element_type=F32)


def gate_up_kernel(groups, g_ref, rows_ref, *refs):
    pieces, out_ref = refs[:-1], refs[-1]
    rows = rows_ref[...].reshape(-1, rows_ref.shape[2])
    for s in range(groups):
        home = lax.rem(g_ref[0] + groups - s, groups)
        out_ref[home] = dot_nt(pieces[s][...], rows).astype(BF16)


def gate_up(g, rows, pieces):
    experts, cap, part = rows.shape
    slots = experts * cap
    groups = len(pieces)
    double = pieces[0].shape[0]
    return pl.pallas_call(
        functools.partial(gate_up_kernel, groups),
        out_shape=jax.ShapeDtypeStruct((groups, double, slots), BF16),
        grid_spec=pltpu.PrefetchScalarGridSpec(
            num_scalar_prefetch=1,
            grid=(1,),
            in_specs=[pl.BlockSpec(rows.shape, lambda i, g_ref: (0, 0, 0))]
            + [pl.BlockSpec((double, part), lambda i, g_ref: (0, 0))] * groups,
            out_specs=pl.BlockSpec((groups, double, slots), lambda i, g_ref: (0, 0, 0)),
        ),
        compiler_params=PARAMS,
        cost_estimate=cost(2 * slots * part * double * groups, 6 << 20),
        name="gate_up",
    )(g, rows, *pieces)


def silu_kernel(acts_ref, out_ref):
    units = out_ref.shape[0]
    gate = jnp.sum(acts_ref[:, :units].astype(F32), axis=0)
    up = jnp.sum(acts_ref[:, units:].astype(F32), axis=0)
    out_ref[...] = (gate / (1.0 + jnp.exp(-gate)) * up).astype(BF16)


def silu(acts):
    _, double, slots = acts.shape
    return pl.pallas_call(
        silu_kernel,
        out_shape=jax.ShapeDtypeStruct((double // 2, slots), BF16),
        in_specs=[VMEM],
        out_specs=VMEM,
        compiler_params=PARAMS,
        cost_estimate=cost(8 * double * slots, 2 << 20),
        name="silu_sum",
    )(acts)


def down_kernel(groups, g_ref, hidden_ref, *refs):
    pieces, out_ref = refs[:-1], refs[-1]
    units, part = pieces[0].shape
    experts, cap, _ = out_ref.shape
    g = g_ref[0]
    chunk = part // 4
    held = [
        hidden_ref[pl.ds(pl.multiple_of(lax.rem(g + groups - s, groups) * units, units), units), :]
        for s in range(groups)
    ]
    for n in range(4):
        columns = slice(n * chunk, (n + 1) * chunk)
        total = dot_tn(held[0], pieces[0][:, columns])
        for s in range(1, groups):
            total += dot_tn(held[s], pieces[s][:, columns])
        out_ref[:, :, columns] = total.astype(BF16).reshape(experts, cap, chunk)


def down(g, hidden, pieces):
    inner, slots = hidden.shape
    groups = len(pieces)
    units, part = inner // groups, pieces[0].shape[1]
    out = (slots // CAP, CAP, part)
    return pl.pallas_call(
        functools.partial(down_kernel, groups),
        out_shape=jax.ShapeDtypeStruct(out, BF16),
        grid_spec=pltpu.PrefetchScalarGridSpec(
            num_scalar_prefetch=1,
            grid=(1,),
            in_specs=[pl.BlockSpec((inner, slots), lambda i, g_ref: (0, 0))]
            + [pl.BlockSpec((units, part), lambda i, g_ref: (0, 0))] * groups,
            out_specs=pl.BlockSpec(out, lambda i, g_ref: (0, 0, 0)),
        ),
        compiler_params=PARAMS,
        cost_estimate=cost(2 * slots * inner * part, 4 << 20),
        name="down",
    )(g, hidden, *pieces)


def combine_kernel(scalar_ref, table_ref, returned_ref, block_ref, known_ref, out_ref):
    _, trees, _ = out_ref.shape
    block, part = block_ref.shape
    tree = block // trees
    returned = returned_ref[...].reshape(-1, part)
    moe = jnp.dot(table_ref[...], returned, preferred_element_type=F32)
    result = (block_ref[...].astype(F32) + moe).astype(BF16).astype(F32)
    place = lax.broadcasted_iota(jnp.int32, (tree, part), 0)
    chosen = []
    for t in range(trees):
        rows = result[t * tree : (t + 1) * tree]
        same = place == scalar_ref[1 + t]
        chosen.append(jnp.sum(jnp.where(same, rows, 0.0), axis=0, keepdims=True))
    chosen = jnp.concatenate(chosen, axis=0)
    lane = lax.broadcasted_iota(jnp.int32, (trees, LINE), 1)
    kept = lax.div(lane, LINE // 2) == lax.rem(scalar_ref[0], 2)
    for q in range(NEAR_SIZE):
        parity, p = divmod(q, P_SIZE)
        first = [(z * P_SIZE + p) * 32 for z in (parity, parity + 2)] * 2
        high = jnp.concatenate([chosen[:, f : f + 32] for f in first], axis=1)
        high = jnp.where(kept, high, 0.0).astype(BF16)
        for j in range(trees):
            d = q * trees + j
            out_ref[d, :, :LINE] = known_ref[q]
            out_ref[d, :, LINE : 2 * LINE] = high
            row = result[j * tree + p : j * tree + p + 1]
            at = parity * part // 2
            lines = [row[:, at + r * LINE : at + (r + 1) * LINE] for r in range(trees)]
            out_ref[d, :, 2 * LINE :] = jnp.concatenate(lines, axis=0).astype(BF16)


def combine(scalars, table, returned, block_in, known):
    block, part = block_in.shape
    trees = known.shape[1]
    return pl.pallas_call(
        combine_kernel,
        out_shape=jax.ShapeDtypeStruct((NEAR_SIZE * trees, trees, 3 * LINE), BF16),
        in_specs=[SMEM] + [VMEM] * 4,
        out_specs=VMEM,
        compiler_params=PARAMS,
        cost_estimate=cost(2 * block * table.shape[1] * part, 2 << 20),
        name="combine",
    )(scalars, table, returned, block_in, known)


def join_kernel(rows_ref, weight_ref, out_ref):
    amount = rows_ref.shape[0]
    trees = amount // NEAR_SIZE
    step = rows_ref.shape[1] // trees
    half = weight_ref.shape[0] // 2

    def line(row, k):
        return rows_ref[:, row * step + k * LINE : row * step + (k + 1) * LINE]

    high = jnp.concatenate([line(t, 1) for t in range(trees)], axis=0)
    row = lax.broadcasted_iota(jnp.int32, (amount, amount * trees), 0)
    column = lax.broadcasted_iota(jnp.int32, (amount, amount * trees), 1)
    place = lax.rem(column, amount)
    same = (lax.div(column, amount) == lax.rem(row, trees)) & (
        lax.div(place, trees) == lax.div(row, trees)
    )
    total = None
    for h in range(2):
        wanted = same & (lax.div(lax.rem(place, trees), 2) == h)
        wanted = jnp.where(wanted, 1.0, 0.0).astype(BF16)
        parts = [
            line(h, 0),
            line(2 + h, 0),
            jnp.dot(wanted, high, preferred_element_type=F32).astype(BF16),
        ]
        for k, values in enumerate(parts):
            weight = weight_ref[h * half : (h + 1) * half, k].reshape(LINE, -1)
            product = jnp.dot(values, weight, preferred_element_type=F32)
            total = product if total is None else total + product
    home = jnp.concatenate([line(r, 2) for r in range(trees)], axis=1).astype(F32)
    wide, narrow = total.shape[1] // 2, home.shape[1] // 2
    for q in range(NEAR_SIZE):
        rows = slice(q * trees, (q + 1) * trees)
        pair = jnp.concatenate([total[rows, :wide], total[rows, wide:]], axis=0)
        out_ref[q, :, :wide] = pair.astype(BF16)
        pair = jnp.concatenate([home[rows, :narrow], home[rows, narrow:]], axis=0)
        out_ref[q, :, wide:] = pair.astype(BF16)


def join(tiles, weight):
    amount, trees, step = tiles.shape
    width = weight.shape[-1]
    shape = (NEAR_SIZE, 2 * trees, width // 2 + trees * LINE // 2)
    return pl.pallas_call(
        join_kernel,
        out_shape=jax.ShapeDtypeStruct(shape, BF16),
        in_specs=[VMEM] * 2,
        out_specs=VMEM,
        compiler_params=PARAMS,
        cost_estimate=cost(2 * amount * weight.size, 4 << 20),
        name="join",
    )(tiles.reshape(amount, trees * step), weight)


def finish_kernel(back_ref, layer_ref, joined_ref):
    _, rows, step = back_ref.shape
    trees, half = joined_ref.shape[0], joined_ref.shape[1] // 2
    narrow = step - half
    summed = jnp.sum(back_ref[:, :, :half].astype(F32), axis=0)
    joined_ref[:, :half] = summed[:trees].astype(BF16)
    joined_ref[:, half:] = summed[trees:].astype(BF16)
    for parity in range(2):
        home = back_ref[parity * P_SIZE : (parity + 1) * P_SIZE, :, half:].astype(F32)
        for r in range(rows):
            lane = (r % trees) * 2 * half + parity * half + (r // trees) * narrow
            layer_ref[:, lane : lane + narrow] = home[:, r, :].astype(BF16)


def finish(back, layer_shape, joined_shape):
    return pl.pallas_call(
        finish_kernel,
        out_shape=[
            jax.ShapeDtypeStruct(layer_shape, BF16),
            jax.ShapeDtypeStruct(joined_shape, BF16),
        ],
        in_specs=[VMEM],
        out_specs=[VMEM] * 2,
        compiler_params=PARAMS,
        cost_estimate=cost(back.size, back.size * 4),
        name="finish",
    )(back)


def route_weights(route_logits):
    exponent = jnp.exp(route_logits)
    return (exponent / jnp.sum(exponent, axis=-1, keepdims=True)).astype(BF16)


def slot_places(route_ids, experts):
    flat_ids = route_ids.reshape(-1)
    amount = flat_ids.shape[0]
    onehot = flat_ids[:, None] == jnp.arange(experts, dtype=jnp.int32)[None, :]
    lower = jnp.arange(amount)[:, None] > jnp.arange(amount)[None, :]
    before = jnp.dot(lower.astype(BF16), onehot.astype(BF16), preferred_element_type=F32)
    rank = jnp.sum(jnp.where(onehot, before, 0.0), axis=1).astype(jnp.int32)
    return flat_ids * CAP + rank


def on_device(
    layer_in,
    norm_gain,
    route_ids,
    route_logits,
    gate_proj,
    up_proj,
    down_proj,
    low_feature,
    mid_feature,
    accepted_node,
    join_weight,
):
    groups = lax.axis_size("y")
    experts = Z_SIZE * P_SIZE
    g = lax.axis_index("y").astype(jnp.int32)
    g_one = g.reshape(1)
    rows_dev, width = layer_in.shape
    block, top = route_ids.shape
    part = width // groups
    slots = experts * CAP
    trees = accepted_node.shape[0]

    join_all = lax.all_gather(join_weight, "zh", axis=0, tiled=False)

    both = normed_and_raw(layer_in, norm_gain, groups)
    both = lax.all_to_all(both, "y", 0, 0, tiled=True)
    block_in = both[:, 1].reshape(block, part)

    weights = route_weights(route_logits)
    places = slot_places(route_ids, experts)
    slot_ids = jnp.arange(slots, dtype=jnp.int32)
    matches = (places[:, None] == slot_ids[None, :]).reshape(block, top, slots)
    dispatch = jnp.any(matches, axis=1).astype(BF16)
    outgoing = dispatch_rows(dispatch, both)

    others = tuple(range(1, groups))
    both_in = [gate_proj, up_proj]
    cut = weight_slices(g_one, both_in, others, groups, "gate_up_slices")
    outgoing, *cut = lax.optimization_barrier((outgoing, *cut))
    gate_up_pieces = [shift_y(piece, groups, s) for s, piece in zip(others, cut)]
    cut = weight_slices(g_one, [down_proj], others, groups, "down_slices")
    down_pieces = [shift_y(piece, groups, s) for s, piece in zip(others, cut)]
    gate_up_pieces = [*weight_slices(g_one, both_in, (0,), groups, "gate_up_own"), *gate_up_pieces]
    down_pieces = [*weight_slices(g_one, [down_proj], (0,), groups, "down_own"), *down_pieces]
    received = lax.all_to_all(outgoing, EXPERT, 0, 0, tiled=True)

    combine_table = jnp.sum(
        jnp.where(matches, weights.astype(F32)[:, :, None], 0.0), axis=1
    ).astype(BF16)

    acts = gate_up(g_one, received, gate_up_pieces)
    acts, *down_pieces = lax.optimization_barrier((acts, *down_pieces))
    acts = lax.all_to_all(acts, "y", 0, 0, tiled=True)
    hidden = silu(acts)
    hidden_all = lax.all_gather(hidden, "y", axis=0, tiled=True)
    expert_out = down(g_one, hidden_all, down_pieces)
    expert_out, join_all = lax.optimization_barrier((expert_out, join_all))
    returned = lax.all_to_all(expert_out, EXPERT, 0, 0, tiled=True)

    own_node = lax.dynamic_slice_in_dim(accepted_node, g, 1, 0)[0]
    feat = width // experts

    def known(feature):
        row = lax.dynamic_index_in_dim(feature, own_node, 0, keepdims=False)
        row = row.reshape(2, Z_SIZE // 4, 2, P_SIZE, feat).transpose(2, 3, 0, 1, 4)
        return row.reshape(NEAR_SIZE, 2, LINE)

    early = jnp.concatenate([known(low_feature), known(mid_feature)], axis=1)
    early, combine_table, block_in, returned = lax.optimization_barrier(
        (early, combine_table, block_in, returned)
    )
    scalars = jnp.concatenate([g_one, accepted_node])
    sent = combine(scalars, combine_table, returned, block_in, early)
    spread = lax.all_to_all(sent, (*NEAR, "y"), 0, 0, tiled=True)

    back = lax.all_to_all(join(spread, join_all), NEAR, 0, 0, tiled=True)
    return tuple(finish(back, (rows_dev, width), (trees, part)))


def solution(mesh):
    every = ("zh", "zl", "p", "y")
    split = Mesh(mesh.devices.reshape(Z_SIZE // 2, 2, P_SIZE, -1), every)
    placed = (
        P(every, None),
        P(),
        P(EXPERT, None),
        P(EXPERT, None),
        P(EXPERT, "y", None),
        P(EXPERT, "y", None),
        P(EXPERT, "y", None),
        P(every, None),
        P(every, None),
        P(EXPERT),
        P(None, EXPERT, "y"),
    )
    return jax.shard_map(
        on_device,
        mesh=split,
        in_specs=placed,
        out_specs=(P(every, None), P(EXPERT, "y")),
        check_vma=False,
    )
```

```python
import functools

import jax
import jax.numpy as jnp
from jax import lax
from jax.experimental import pallas as pl
from jax.experimental.pallas import tpu as pltpu
from jax.sharding import Mesh
from jax.sharding import PartitionSpec as P

EPSILON = 1e-06
Z_SIZE = 16
P_SIZE = 8
CAP = 4
EXPERT = ("z", "p")
F32 = jnp.float32
BF16 = jnp.bfloat16
PARAMS = pltpu.CompilerParams(vmem_limit_bytes=40 * 1024 * 1024)
VMEM = pl.BlockSpec(memory_space=pltpu.VMEM)
SMEM = pl.BlockSpec(memory_space=pltpu.SMEM)


def shift_y(array, groups, shift):
    return lax.ppermute(array, "y", [(j, (j + shift) % groups) for j in range(groups)])


def cost(flops, moved):
    return pl.CostEstimate(flops=flops, bytes_accessed=moved, transcendentals=0)


def norm_kernel(layer_ref, gain_ref, out_ref):
    groups, _, _, part = out_ref.shape
    widened = layer_ref[...].astype(F32)
    inverse = lax.rsqrt(jnp.mean(widened * widened, axis=-1, keepdims=True) + EPSILON)
    gain = gain_ref[...].reshape(1, -1).astype(F32)
    normed = (widened * inverse * gain).astype(BF16)
    for j in range(groups):
        out_ref[j, 0] = normed[:, j * part : (j + 1) * part]
        out_ref[j, 1] = layer_ref[:, j * part : (j + 1) * part]


def normed_and_raw(layer_in, norm_gain, groups):
    rows, width = layer_in.shape
    return pl.pallas_call(
        norm_kernel,
        out_shape=jax.ShapeDtypeStruct((groups, 2, rows, width // groups), BF16),
        in_specs=[VMEM] * 2,
        out_specs=VMEM,
        compiler_params=PARAMS,
        cost_estimate=cost(rows * width * 6, rows * width * 6),
        name="norm_pack",
    )(layer_in, norm_gain)


def slice_kernel(plan, groups, g_ref, *refs):
    sources, outs, sems = refs[:3], refs[3:-1], refs[-1]
    part = sources[0].shape[2] // groups
    copies = []
    for i, (out, moves) in enumerate(zip(outs, plan)):
        at = 0
        for k, (source, first, amount, shift) in enumerate(moves):
            lane = pl.multiple_of(lax.rem(g_ref[0] + shift, groups) * part, part)
            copies.append(
                pltpu.make_async_copy(
                    sources[source].at[0, pl.ds(first, amount), pl.ds(lane, part)],
                    out.at[pl.ds(at, amount), :],
                    sems.at[i, k],
                )
            )
            at += amount
    for copy in copies:
        copy.start()
    for copy in copies:
        copy.wait()


def weight_slices(g, sources, plan, groups, name):
    part = sources[0].shape[2] // groups
    rows = [sum(amount for _, _, amount, _ in moves) for moves in plan]
    return pl.pallas_call(
        functools.partial(slice_kernel, plan, groups),
        out_shape=[jax.ShapeDtypeStruct((amount, part), BF16) for amount in rows],
        in_specs=[SMEM] + [pl.BlockSpec(memory_space=pltpu.HBM)] * 3,
        out_specs=[VMEM] * len(plan),
        scratch_shapes=[pltpu.SemaphoreType.DMA((len(plan), max(len(m) for m in plan)))],
        compiler_params=pltpu.CompilerParams(vmem_limit_bytes=60 * 1024 * 1024),
        cost_estimate=cost(0, 4 * sum(rows) * part),
        name=name,
    )(g, *sources)


def dispatch_kernel(table_ref, both_ref, out_ref):
    part = both_ref.shape[3]
    normed = both_ref[:, 0].reshape(-1, part)
    rows = dot_tn(table_ref[...], normed).astype(BF16)
    out_ref[...] = rows.reshape(out_ref.shape)


def dispatch_rows(table, both):
    part = both.shape[3]
    slots = table.shape[1]
    return pl.pallas_call(
        dispatch_kernel,
        out_shape=jax.ShapeDtypeStruct((slots // CAP, CAP, part), BF16),
        in_specs=[VMEM] * 2,
        out_specs=VMEM,
        compiler_params=PARAMS,
        cost_estimate=cost(2 * table.size * part, 2 * slots * part),
        name="dispatch",
    )(table, both)


def dot_nt(a, b):
    return lax.dot_general(a, b, (((1,), (1,)), ((), ())), preferred_element_type=F32)


def dot_tn(a, b):
    return lax.dot_general(a, b, (((0,), (0,)), ((), ())), preferred_element_type=F32)


def gate_up_kernel(groups, g_ref, rows_ref, *refs):
    pieces, out_ref = refs[:-1], refs[-1]
    rows = rows_ref[...].reshape(-1, rows_ref.shape[2])
    for s in range(groups):
        home = lax.rem(g_ref[0] + groups - s, groups)
        out_ref[home] = dot_nt(pieces[s][...], rows).astype(BF16)


def gate_up(g, rows, pieces):
    experts, cap, part = rows.shape
    slots = experts * cap
    groups = len(pieces)
    double = pieces[1].shape[0]
    return pl.pallas_call(
        functools.partial(gate_up_kernel, groups),
        out_shape=jax.ShapeDtypeStruct((groups, double, slots), BF16),
        grid_spec=pltpu.PrefetchScalarGridSpec(
            num_scalar_prefetch=1,
            grid=(1,),
            in_specs=[pl.BlockSpec(rows.shape, lambda i, g_ref: (0, 0, 0))]
            + [pl.BlockSpec((double, part), lambda i, g_ref: (0, 0))] * groups,
            out_specs=pl.BlockSpec((groups, double, slots), lambda i, g_ref: (0, 0, 0)),
        ),
        compiler_params=PARAMS,
        cost_estimate=cost(2 * slots * part * double * groups, 6 << 20),
        name="gate_up",
    )(g, rows, *pieces)


def silu_kernel(acts_ref, out_ref):
    units = out_ref.shape[0]
    gate = jnp.sum(acts_ref[:, :units].astype(F32), axis=0)
    up = jnp.sum(acts_ref[:, units:].astype(F32), axis=0)
    out_ref[...] = (gate / (1.0 + jnp.exp(-gate)) * up).astype(BF16)


def silu(acts):
    _, double, slots = acts.shape
    return pl.pallas_call(
        silu_kernel,
        out_shape=jax.ShapeDtypeStruct((double // 2, slots), BF16),
        in_specs=[VMEM],
        out_specs=VMEM,
        compiler_params=PARAMS,
        cost_estimate=cost(8 * double * slots, 2 << 20),
        name="silu_sum",
    )(acts)


def down_kernel(groups, g_ref, hidden_ref, *refs):
    pieces, out_ref = refs[:-1], refs[-1]
    units, part = pieces[0].shape
    experts, cap, _ = out_ref.shape
    g = g_ref[0]
    chunk = part // 4
    held = [
        hidden_ref[pl.ds(pl.multiple_of(lax.rem(g + groups - s, groups) * units, units), units), :]
        for s in range(groups)
    ]
    for n in range(4):
        columns = slice(n * chunk, (n + 1) * chunk)
        total = dot_tn(held[0], pieces[0][:, columns])
        for s in range(1, groups):
            total += dot_tn(held[s], pieces[s][:, columns])
        out_ref[:, :, columns] = total.astype(BF16).reshape(experts, cap, chunk)


def down(g, hidden, pieces):
    inner, slots = hidden.shape
    groups = len(pieces)
    units, part = inner // groups, pieces[0].shape[1]
    out = (slots // CAP, CAP, part)
    return pl.pallas_call(
        functools.partial(down_kernel, groups),
        out_shape=jax.ShapeDtypeStruct(out, BF16),
        grid_spec=pltpu.PrefetchScalarGridSpec(
            num_scalar_prefetch=1,
            grid=(1,),
            in_specs=[pl.BlockSpec((inner, slots), lambda i, g_ref: (0, 0))]
            + [
                pl.BlockSpec((units, part), lambda i, g_ref, k=piece.shape[0] // units - 1: (k, 0))
                for piece in pieces
            ],
            out_specs=pl.BlockSpec(out, lambda i, g_ref: (0, 0, 0)),
        ),
        compiler_params=PARAMS,
        cost_estimate=cost(2 * slots * inner * part, 4 << 20),
        name="down",
    )(g, hidden, *pieces)


def combine_kernel(node_ref, table_ref, returned_ref, block_ref, known_ref, out_ref):
    dests, trees, _ = out_ref.shape
    block, part = block_ref.shape
    peers = part // 128
    groups = dests // peers
    tree = block // trees
    zs = known_ref.shape[2] // 2 // 32
    returned = returned_ref[...].reshape(-1, part)
    moe = jnp.dot(table_ref[...], returned, preferred_element_type=F32)
    result = (block_ref[...].astype(F32) + moe).astype(BF16).astype(F32)
    place = lax.broadcasted_iota(jnp.int32, (tree, part), 0)
    chosen = []
    for t in range(trees):
        rows = result[t * tree : (t + 1) * tree]
        chosen.append(jnp.sum(jnp.where(place == node_ref[t], rows, 0.0), axis=0, keepdims=True))
    chosen = jnp.concatenate(chosen, axis=0)
    for p in range(peers):
        parts = [chosen[:, z * peers * 32 + p * 32 : z * peers * 32 + p * 32 + 32] for z in range(zs)]
        high = jnp.concatenate(parts, axis=1).astype(BF16)
        lanes = slice(p * 128, p * 128 + 128)
        for j in range(groups):
            d = p * groups + j
            out_ref[d, :, 0:256] = known_ref[p]
            out_ref[d, :, 256:384] = high
            rows = result[j * tree : (j + 1) * tree, lanes]
            out_ref[d, :, 384:512] = rows[:trees].astype(BF16)
            out_ref[d, :, 512:640] = rows[trees:].astype(BF16)


def combine(nodes, table, returned, block_in, known, dests):
    block, part = block_in.shape
    trees = nodes.shape[0]
    return pl.pallas_call(
        combine_kernel,
        out_shape=jax.ShapeDtypeStruct((dests, trees, 640), BF16),
        in_specs=[SMEM] + [VMEM] * 4,
        out_specs=VMEM,
        compiler_params=PARAMS,
        cost_estimate=cost(2 * block * table.shape[1] * part, 2 << 20),
        name="combine",
    )(nodes, table, returned, block_in, known)


def join_kernel(rows_ref, tiles_ref, weight_ref, out_ref):
    amount, trees, step = tiles_ref.shape
    peers = out_ref.shape[0]
    line = 128
    quarter = weight_ref.shape[0] // trees
    high = jnp.concatenate(
        [rows_ref[:, t * step + 2 * line : t * step + 3 * line] for t in range(trees)], axis=0
    )
    row = lax.broadcasted_iota(jnp.int32, (amount, amount * trees), 0)
    column = lax.broadcasted_iota(jnp.int32, (amount, amount * trees), 1)
    place = lax.rem(column, amount)
    same = (lax.div(column, amount) == lax.rem(row, trees)) & (
        lax.div(place, trees) == lax.div(row, trees)
    )
    total = None
    for q in range(trees):
        chosen = jnp.where(same & (lax.rem(place, trees) == q), 1.0, 0.0).astype(BF16)
        parts = [
            rows_ref[:, q * step : q * step + line],
            rows_ref[:, q * step + line : q * step + 2 * line],
            jnp.dot(chosen, high, preferred_element_type=F32).astype(BF16),
        ]
        for k, values in enumerate(parts):
            weight = weight_ref[q * quarter : (q + 1) * quarter, k].reshape(line, -1)
            product = jnp.dot(values, weight, preferred_element_type=F32)
            total = product if total is None else total + product
    half = total.shape[1] // 2
    for p in range(peers):
        rows = slice(p * trees, (p + 1) * trees)
        pair = jnp.concatenate([total[rows, :half], total[rows, half:]], axis=0)
        out_ref[p, 0 : 2 * trees] = pair.astype(BF16)
        for j in range(trees):
            for h in range(2):
                lanes = slice((3 + h) * line, (4 + h) * line)
                out_ref[p, (2 + h) * trees : (3 + h) * trees, j * line : (j + 1) * line] = (
                    tiles_ref[p * trees + j, :, lanes]
                )


def join(tiles, weight):
    amount, trees, step = tiles.shape
    peers = amount // trees
    width = weight.shape[-1]
    return pl.pallas_call(
        join_kernel,
        out_shape=jax.ShapeDtypeStruct((peers, 4 * trees, width // 2), BF16),
        in_specs=[VMEM] * 3,
        out_specs=VMEM,
        compiler_params=PARAMS,
        cost_estimate=cost(2 * amount * weight.size, 4 << 20),
        name="join",
    )(tiles.reshape(amount, trees * step), tiles, weight)


def finish_kernel(back_ref, layer_ref, joined_ref):
    peers, rows, half = back_ref.shape
    trees = rows // 4
    summed = jnp.sum(back_ref[:, 0 : 2 * trees].astype(F32), axis=0)
    joined_ref[:, :half] = summed[:trees].astype(BF16)
    joined_ref[:, half:] = summed[trees:].astype(BF16)
    for p in range(peers):
        for j in range(trees):
            lane = j * 2 * half + p * 128
            layer_ref[:, lane : lane + 128] = back_ref[
                p, 2 * trees : 4 * trees, j * 128 : (j + 1) * 128
            ]


def finish(back, layer_shape, joined_shape):
    return pl.pallas_call(
        finish_kernel,
        out_shape=[
            jax.ShapeDtypeStruct(layer_shape, BF16),
            jax.ShapeDtypeStruct(joined_shape, BF16),
        ],
        in_specs=[VMEM],
        out_specs=[VMEM] * 2,
        compiler_params=PARAMS,
        cost_estimate=cost(back.size, back.size * 4),
        name="finish",
    )(back)


def route_weights(route_logits):
    exponent = jnp.exp(route_logits)
    return (exponent / jnp.sum(exponent, axis=-1, keepdims=True)).astype(BF16)


def slot_places(route_ids, experts):
    flat_ids = route_ids.reshape(-1)
    amount = flat_ids.shape[0]
    onehot = flat_ids[:, None] == jnp.arange(experts, dtype=jnp.int32)[None, :]
    lower = jnp.arange(amount)[:, None] > jnp.arange(amount)[None, :]
    before = jnp.dot(lower.astype(BF16), onehot.astype(BF16), preferred_element_type=F32)
    rank = jnp.sum(jnp.where(onehot, before, 0.0), axis=1).astype(jnp.int32)
    return flat_ids * CAP + rank


def on_device(
    layer_in,
    norm_gain,
    route_ids,
    route_logits,
    gate_proj,
    up_proj,
    down_proj,
    low_feature,
    mid_feature,
    accepted_node,
    join_weight,
):
    groups = lax.axis_size("y")
    experts = Z_SIZE * P_SIZE
    g = lax.axis_index("y").astype(jnp.int32)
    g_one = g.reshape(1)
    rows_dev, width = layer_in.shape
    block, top = route_ids.shape
    part = width // groups
    slots = experts * CAP
    trees = accepted_node.shape[0]

    join_all = lax.all_gather(join_weight, "z", axis=0, tiled=False)

    both = normed_and_raw(layer_in, norm_gain, groups)
    both = lax.all_to_all(both, "y", 0, 0, tiled=True)
    block_in = both[:, 1].reshape(block, part)

    weights = route_weights(route_logits)
    places = slot_places(route_ids, experts)
    slot_ids = jnp.arange(slots, dtype=jnp.int32)
    matches = (places[:, None] == slot_ids[None, :]).reshape(block, top, slots)
    dispatch = jnp.any(matches, axis=1).astype(BF16)
    outgoing = dispatch_rows(dispatch, both)

    units = gate_proj.shape[1]
    sources = [gate_proj, up_proj, down_proj]

    def plan(shift, kinds):
        return [(kind, 0, units, shift) for kind in kinds]

    cut = [plan(1, (0, 1)), plan(2, (0, 1, 2)), plan(3, (0, 1))]
    cut = weight_slices(g_one, sources, cut, groups, "first_slices")
    outgoing, *cut = lax.optimization_barrier((outgoing, *cut))
    near = [shift_y(cut[0], groups, 1), shift_y(cut[2], groups, 3)]
    far = shift_y(cut[1], groups, 2)
    cut = weight_slices(g_one, sources, [plan(1, (2,)), plan(3, (2,))], groups, "down_slices")
    near_down = [shift_y(cut[0], groups, 1), shift_y(cut[1], groups, 3)]
    (own,) = weight_slices(g_one, sources, [plan(0, (0, 1, 2))], groups, "own_slices")
    gate_up_pieces = [own, near[0], far, near[1]]
    down_pieces = [own, near_down[0], far, near_down[1]]
    received = lax.all_to_all(outgoing, EXPERT, 0, 0, tiled=True)

    combine_table = jnp.sum(
        jnp.where(matches, weights.astype(F32)[:, :, None], 0.0), axis=1
    ).astype(BF16)

    acts = gate_up(g_one, received, gate_up_pieces)
    acts, down_pieces[1], down_pieces[3] = lax.optimization_barrier(
        (acts, down_pieces[1], down_pieces[3])
    )
    acts = lax.all_to_all(acts, "y", 0, 0, tiled=True)
    hidden = silu(acts)
    hidden_all = lax.all_gather(hidden, "y", axis=0, tiled=True)
    expert_out = down(g_one, hidden_all, down_pieces)
    returned = lax.all_to_all(expert_out, EXPERT, 0, 0, tiled=True)

    own_node = lax.dynamic_slice_in_dim(accepted_node, g, 1, 0)[0]
    feat = width // experts
    z_part = Z_SIZE // groups

    def known(feature):
        row = lax.dynamic_index_in_dim(feature, own_node, 0, keepdims=False)
        row = row.reshape(groups, z_part, P_SIZE, feat).transpose(2, 0, 1, 3)
        return row.reshape(P_SIZE, groups, z_part * feat)

    early = jnp.concatenate([known(low_feature), known(mid_feature)], axis=-1)
    early, combine_table, block_in, join_all, returned = lax.optimization_barrier(
        (early, combine_table, block_in, join_all, returned)
    )
    sent = combine(accepted_node, combine_table, returned, block_in, early, P_SIZE * groups)
    spread = lax.all_to_all(sent, ("p", "y"), 0, 0, tiled=True)

    back = lax.all_to_all(join(spread, join_all), "p", 0, 0, tiled=True)
    return tuple(finish(back, (rows_dev, width), (trees, part)))


def solution(mesh):
    split = Mesh(mesh.devices.reshape(Z_SIZE, P_SIZE, -1), ("z", "p", "y"))
    every = ("z", "p", "y")
    placed = (
        P(every, None),
        P(),
        P(EXPERT, None),
        P(EXPERT, None),
        P(EXPERT, "y", None),
        P(EXPERT, "y", None),
        P(EXPERT, "y", None),
        P(every, None),
        P(every, None),
        P(EXPERT),
        P(None, EXPERT, "y"),
    )
    return jax.shard_map(
        on_device,
        mesh=split,
        in_specs=placed,
        out_specs=(P(every, None), P(EXPERT, "y")),
        check_vma=False,
    )
```

```python
import functools

import jax
import jax.numpy as jnp
from jax import lax
from jax.experimental import pallas as pl
from jax.experimental.pallas import tpu as pltpu
from jax.sharding import Mesh
from jax.sharding import PartitionSpec as P

EPSILON = 1e-06
Z_SIZE = 16
P_SIZE = 8
CAP = 4
EXPERT = ("z", "p")
F32 = jnp.float32
BF16 = jnp.bfloat16
PARAMS = pltpu.CompilerParams(vmem_limit_bytes=40 * 1024 * 1024)
VMEM = pl.BlockSpec(memory_space=pltpu.VMEM)
SMEM = pl.BlockSpec(memory_space=pltpu.SMEM)


def shift_y(array, groups, shift):
    return lax.ppermute(array, "y", [(j, (j + shift) % groups) for j in range(groups)])


def cost(flops, moved):
    return pl.CostEstimate(flops=flops, bytes_accessed=moved, transcendentals=0)


def norm_kernel(layer_ref, gain_ref, out_ref):
    groups, _, _, part = out_ref.shape
    widened = layer_ref[...].astype(F32)
    inverse = lax.rsqrt(jnp.mean(widened * widened, axis=-1, keepdims=True) + EPSILON)
    gain = gain_ref[...].reshape(1, -1).astype(F32)
    normed = (widened * inverse * gain).astype(BF16)
    for j in range(groups):
        out_ref[j, 0] = normed[:, j * part : (j + 1) * part]
        out_ref[j, 1] = layer_ref[:, j * part : (j + 1) * part]


def normed_and_raw(layer_in, norm_gain, groups):
    rows, width = layer_in.shape
    return pl.pallas_call(
        norm_kernel,
        out_shape=jax.ShapeDtypeStruct((groups, 2, rows, width // groups), BF16),
        in_specs=[VMEM] * 2,
        out_specs=VMEM,
        compiler_params=PARAMS,
        cost_estimate=cost(rows * width * 6, rows * width * 6),
        name="norm_pack",
    )(layer_in, norm_gain)


def slice_kernel(plan, groups, g_ref, *refs):
    sources, outs, sems = refs[:3], refs[3:-1], refs[-1]
    part = sources[0].shape[2] // groups
    copies = []
    for i, (out, moves) in enumerate(zip(outs, plan)):
        at = 0
        for k, (source, first, amount, shift) in enumerate(moves):
            lane = pl.multiple_of(lax.rem(g_ref[0] + shift, groups) * part, part)
            copies.append(
                pltpu.make_async_copy(
                    sources[source].at[0, pl.ds(first, amount), pl.ds(lane, part)],
                    out.at[pl.ds(at, amount), :],
                    sems.at[i, k],
                )
            )
            at += amount
    for copy in copies:
        copy.start()
    for copy in copies:
        copy.wait()


def weight_slices(g, sources, plan, groups, name):
    part = sources[0].shape[2] // groups
    rows = [sum(amount for _, _, amount, _ in moves) for moves in plan]
    return pl.pallas_call(
        functools.partial(slice_kernel, plan, groups),
        out_shape=[jax.ShapeDtypeStruct((amount, part), BF16) for amount in rows],
        in_specs=[SMEM] + [pl.BlockSpec(memory_space=pltpu.HBM)] * 3,
        out_specs=[VMEM] * len(plan),
        scratch_shapes=[pltpu.SemaphoreType.DMA((len(plan), max(len(m) for m in plan)))],
        compiler_params=pltpu.CompilerParams(vmem_limit_bytes=60 * 1024 * 1024),
        cost_estimate=cost(0, 4 * sum(rows) * part),
        name=name,
    )(g, *sources)


def dispatch_kernel(table_ref, both_ref, out_ref):
    part = both_ref.shape[3]
    normed = both_ref[:, 0].reshape(-1, part)
    rows = dot_tn(table_ref[...], normed).astype(BF16)
    out_ref[...] = rows.reshape(out_ref.shape)


def dispatch_rows(table, both):
    part = both.shape[3]
    slots = table.shape[1]
    return pl.pallas_call(
        dispatch_kernel,
        out_shape=jax.ShapeDtypeStruct((slots // CAP, CAP, part), BF16),
        in_specs=[VMEM] * 2,
        out_specs=VMEM,
        compiler_params=PARAMS,
        cost_estimate=cost(2 * table.size * part, 2 * slots * part),
        name="dispatch",
    )(table, both)


def dot_nt(a, b):
    return lax.dot_general(a, b, (((1,), (1,)), ((), ())), preferred_element_type=F32)


def dot_tn(a, b):
    return lax.dot_general(a, b, (((0,), (0,)), ((), ())), preferred_element_type=F32)


def gate_up_kernel(groups, g_ref, rows_ref, *refs):
    pieces, out_ref = refs[:-1], refs[-1]
    rows = rows_ref[...].reshape(-1, rows_ref.shape[2])
    for s in range(groups):
        home = lax.rem(g_ref[0] + groups - s, groups)
        out_ref[home] = dot_nt(pieces[s][...], rows).astype(BF16)


def gate_up(g, rows, pieces):
    experts, cap, part = rows.shape
    slots = experts * cap
    groups = len(pieces)
    double = pieces[1].shape[0]
    return pl.pallas_call(
        functools.partial(gate_up_kernel, groups),
        out_shape=jax.ShapeDtypeStruct((groups, double, slots), BF16),
        grid_spec=pltpu.PrefetchScalarGridSpec(
            num_scalar_prefetch=1,
            grid=(1,),
            in_specs=[pl.BlockSpec(rows.shape, lambda i, g_ref: (0, 0, 0))]
            + [pl.BlockSpec((double, part), lambda i, g_ref: (0, 0))] * groups,
            out_specs=pl.BlockSpec((groups, double, slots), lambda i, g_ref: (0, 0, 0)),
        ),
        compiler_params=PARAMS,
        cost_estimate=cost(2 * slots * part * double * groups, 6 << 20),
        name="gate_up",
    )(g, rows, *pieces)


def silu_kernel(acts_ref, out_ref):
    units = out_ref.shape[0]
    gate = jnp.sum(acts_ref[:, :units].astype(F32), axis=0)
    up = jnp.sum(acts_ref[:, units:].astype(F32), axis=0)
    out_ref[...] = (gate / (1.0 + jnp.exp(-gate)) * up).astype(BF16)


def silu(acts):
    _, double, slots = acts.shape
    return pl.pallas_call(
        silu_kernel,
        out_shape=jax.ShapeDtypeStruct((double // 2, slots), BF16),
        in_specs=[VMEM],
        out_specs=VMEM,
        compiler_params=PARAMS,
        cost_estimate=cost(8 * double * slots, 2 << 20),
        name="silu_sum",
    )(acts)


def down_kernel(groups, g_ref, hidden_ref, *refs):
    pieces, out_ref = refs[:-1], refs[-1]
    units, part = pieces[0].shape
    experts, cap, _ = out_ref.shape
    g = g_ref[0]
    chunk = part // 4
    held = [
        hidden_ref[pl.ds(pl.multiple_of(lax.rem(g + groups - s, groups) * units, units), units), :]
        for s in range(groups)
    ]
    for n in range(4):
        columns = slice(n * chunk, (n + 1) * chunk)
        total = dot_tn(held[0], pieces[0][:, columns])
        for s in range(1, groups):
            total += dot_tn(held[s], pieces[s][:, columns])
        out_ref[:, :, columns] = total.astype(BF16).reshape(experts, cap, chunk)


def down(g, hidden, pieces):
    inner, slots = hidden.shape
    groups = len(pieces)
    units, part = inner // groups, pieces[0].shape[1]
    out = (slots // CAP, CAP, part)
    return pl.pallas_call(
        functools.partial(down_kernel, groups),
        out_shape=jax.ShapeDtypeStruct(out, BF16),
        grid_spec=pltpu.PrefetchScalarGridSpec(
            num_scalar_prefetch=1,
            grid=(1,),
            in_specs=[pl.BlockSpec((inner, slots), lambda i, g_ref: (0, 0))]
            + [
                pl.BlockSpec((units, part), lambda i, g_ref, k=piece.shape[0] // units - 1: (k, 0))
                for piece in pieces
            ],
            out_specs=pl.BlockSpec(out, lambda i, g_ref: (0, 0, 0)),
        ),
        compiler_params=PARAMS,
        cost_estimate=cost(2 * slots * inner * part, 4 << 20),
        name="down",
    )(g, hidden, *pieces)


def combine_kernel(node_ref, table_ref, returned_ref, block_ref, known_ref, out_ref):
    dests, trees, _ = out_ref.shape
    block, part = block_ref.shape
    peers = part // 128
    groups = dests // peers
    tree = block // trees
    zs = known_ref.shape[2] // 2 // 32
    returned = returned_ref[...].reshape(-1, part)
    moe = jnp.dot(table_ref[...], returned, preferred_element_type=F32)
    result = (block_ref[...].astype(F32) + moe).astype(BF16).astype(F32)
    place = lax.broadcasted_iota(jnp.int32, (tree, part), 0)
    chosen = []
    for t in range(trees):
        rows = result[t * tree : (t + 1) * tree]
        chosen.append(jnp.sum(jnp.where(place == node_ref[t], rows, 0.0), axis=0, keepdims=True))
    chosen = jnp.concatenate(chosen, axis=0)
    for p in range(peers):
        parts = [chosen[:, z * peers * 32 + p * 32 : z * peers * 32 + p * 32 + 32] for z in range(zs)]
        high = jnp.concatenate(parts, axis=1).astype(BF16)
        lanes = slice(p * 128, p * 128 + 128)
        for j in range(groups):
            d = p * groups + j
            out_ref[d, :, 0:256] = known_ref[p]
            out_ref[d, :, 256:384] = high
            rows = result[j * tree : (j + 1) * tree, lanes]
            out_ref[d, :, 384:512] = rows[:trees].astype(BF16)
            out_ref[d, :, 512:640] = rows[trees:].astype(BF16)


def combine(nodes, table, returned, block_in, known, dests):
    block, part = block_in.shape
    trees = nodes.shape[0]
    return pl.pallas_call(
        combine_kernel,
        out_shape=jax.ShapeDtypeStruct((dests, trees, 640), BF16),
        in_specs=[SMEM] + [VMEM] * 4,
        out_specs=VMEM,
        compiler_params=PARAMS,
        cost_estimate=cost(2 * block * table.shape[1] * part, 2 << 20),
        name="combine",
    )(nodes, table, returned, block_in, known)


def held_kernel(weight_ref, out_ref):
    out_ref[...] = weight_ref[...]


def held(weight):
    return pl.pallas_call(
        held_kernel,
        out_shape=jax.ShapeDtypeStruct(weight.shape, BF16),
        in_specs=[VMEM],
        out_specs=VMEM,
        compiler_params=PARAMS,
        cost_estimate=cost(0, 4 * weight.size),
        name="held",
    )(weight)


def join_kernel(rows_ref, tiles_ref, weight_ref, out_ref):
    amount, trees, step = tiles_ref.shape
    peers = out_ref.shape[0]
    line = 128
    quarter = weight_ref.shape[0] // trees
    high = jnp.concatenate(
        [rows_ref[:, t * step + 2 * line : t * step + 3 * line] for t in range(trees)], axis=0
    )
    row = lax.broadcasted_iota(jnp.int32, (amount, amount * trees), 0)
    column = lax.broadcasted_iota(jnp.int32, (amount, amount * trees), 1)
    place = lax.rem(column, amount)
    same = (lax.div(column, amount) == lax.rem(row, trees)) & (
        lax.div(place, trees) == lax.div(row, trees)
    )
    total = None
    for q in range(trees):
        chosen = jnp.where(same & (lax.rem(place, trees) == q), 1.0, 0.0).astype(BF16)
        parts = [
            rows_ref[:, q * step : q * step + line],
            rows_ref[:, q * step + line : q * step + 2 * line],
            jnp.dot(chosen, high, preferred_element_type=F32).astype(BF16),
        ]
        for k, values in enumerate(parts):
            weight = weight_ref[q * quarter : (q + 1) * quarter, k].reshape(line, -1)
            product = jnp.dot(values, weight, preferred_element_type=F32)
            total = product if total is None else total + product
    half = total.shape[1] // 2
    for p in range(peers):
        rows = slice(p * trees, (p + 1) * trees)
        pair = jnp.concatenate([total[rows, :half], total[rows, half:]], axis=0)
        out_ref[p, 0 : 2 * trees] = pair.astype(BF16)
        for j in range(trees):
            for h in range(2):
                lanes = slice((3 + h) * line, (4 + h) * line)
                out_ref[p, (2 + h) * trees : (3 + h) * trees, j * line : (j + 1) * line] = (
                    tiles_ref[p * trees + j, :, lanes]
                )


def join(tiles, weight):
    amount, trees, step = tiles.shape
    peers = amount // trees
    width = weight.shape[-1]
    return pl.pallas_call(
        join_kernel,
        out_shape=jax.ShapeDtypeStruct((peers, 4 * trees, width // 2), BF16),
        in_specs=[VMEM] * 3,
        out_specs=VMEM,
        compiler_params=PARAMS,
        cost_estimate=cost(2 * amount * weight.size, 4 << 20),
        name="join",
    )(tiles.reshape(amount, trees * step), tiles, weight)


def finish_kernel(back_ref, layer_ref, joined_ref):
    peers, rows, half = back_ref.shape
    trees = rows // 4
    summed = jnp.sum(back_ref[:, 0 : 2 * trees].astype(F32), axis=0)
    joined_ref[:, :half] = summed[:trees].astype(BF16)
    joined_ref[:, half:] = summed[trees:].astype(BF16)
    for p in range(peers):
        for j in range(trees):
            lane = j * 2 * half + p * 128
            layer_ref[:, lane : lane + 128] = back_ref[
                p, 2 * trees : 4 * trees, j * 128 : (j + 1) * 128
            ]


def finish(back, layer_shape, joined_shape):
    return pl.pallas_call(
        finish_kernel,
        out_shape=[
            jax.ShapeDtypeStruct(layer_shape, BF16),
            jax.ShapeDtypeStruct(joined_shape, BF16),
        ],
        in_specs=[VMEM],
        out_specs=[VMEM] * 2,
        compiler_params=PARAMS,
        cost_estimate=cost(back.size, back.size * 4),
        name="finish",
    )(back)


def route_weights(route_logits):
    exponent = jnp.exp(route_logits)
    return (exponent / jnp.sum(exponent, axis=-1, keepdims=True)).astype(BF16)


def slot_places(route_ids, experts):
    flat_ids = route_ids.reshape(-1)
    amount = flat_ids.shape[0]
    onehot = flat_ids[:, None] == jnp.arange(experts, dtype=jnp.int32)[None, :]
    lower = jnp.arange(amount)[:, None] > jnp.arange(amount)[None, :]
    before = jnp.dot(lower.astype(BF16), onehot.astype(BF16), preferred_element_type=F32)
    rank = jnp.sum(jnp.where(onehot, before, 0.0), axis=1).astype(jnp.int32)
    return flat_ids * CAP + rank


def on_device(
    layer_in,
    norm_gain,
    route_ids,
    route_logits,
    gate_proj,
    up_proj,
    down_proj,
    low_feature,
    mid_feature,
    accepted_node,
    join_weight,
):
    groups = lax.axis_size("y")
    experts = Z_SIZE * P_SIZE
    g = lax.axis_index("y").astype(jnp.int32)
    g_one = g.reshape(1)
    rows_dev, width = layer_in.shape
    block, top = route_ids.shape
    part = width // groups
    slots = experts * CAP
    trees = accepted_node.shape[0]

    join_all = lax.all_gather(join_weight, "z", axis=0, tiled=False)

    both = normed_and_raw(layer_in, norm_gain, groups)
    both = lax.all_to_all(both, "y", 0, 0, tiled=True)
    block_in = both[:, 1].reshape(block, part)

    weights = route_weights(route_logits)
    places = slot_places(route_ids, experts)
    slot_ids = jnp.arange(slots, dtype=jnp.int32)
    matches = (places[:, None] == slot_ids[None, :]).reshape(block, top, slots)
    dispatch = jnp.any(matches, axis=1).astype(BF16)
    outgoing = dispatch_rows(dispatch, both)

    units = gate_proj.shape[1]
    sources = [gate_proj, up_proj, down_proj]

    def plan(shift, kinds):
        return [(kind, 0, units, shift) for kind in kinds]

    cut = [plan(1, (0, 1)), plan(2, (0, 1, 2)), plan(3, (0, 1))]
    cut = weight_slices(g_one, sources, cut, groups, "first_slices")
    outgoing, *cut = lax.optimization_barrier((outgoing, *cut))
    near = [shift_y(cut[0], groups, 1), shift_y(cut[2], groups, 3)]
    far = shift_y(cut[1], groups, 2)
    cut = weight_slices(g_one, sources, [plan(1, (2,)), plan(3, (2,))], groups, "down_slices")
    near_down = [shift_y(cut[0], groups, 1), shift_y(cut[1], groups, 3)]
    (own,) = weight_slices(g_one, sources, [plan(0, (0, 1, 2))], groups, "own_slices")
    gate_up_pieces = [own, near[0], far, near[1]]
    down_pieces = [own, near_down[0], far, near_down[1]]
    received = lax.all_to_all(outgoing, EXPERT, 0, 0, tiled=True)

    combine_table = jnp.sum(
        jnp.where(matches, weights.astype(F32)[:, :, None], 0.0), axis=1
    ).astype(BF16)

    acts = gate_up(g_one, received, gate_up_pieces)
    acts, down_pieces[1], down_pieces[3] = lax.optimization_barrier(
        (acts, down_pieces[1], down_pieces[3])
    )
    acts = lax.all_to_all(acts, "y", 0, 0, tiled=True)
    hidden = silu(acts)
    hidden_all = lax.all_gather(hidden, "y", axis=0, tiled=True)
    expert_out = down(g_one, hidden_all, down_pieces)
    returned = lax.all_to_all(expert_out, EXPERT, 0, 0, tiled=True)

    own_node = lax.dynamic_slice_in_dim(accepted_node, g, 1, 0)[0]
    feat = width // experts
    z_part = Z_SIZE // groups

    def known(feature):
        row = lax.dynamic_index_in_dim(feature, own_node, 0, keepdims=False)
        row = row.reshape(groups, z_part, P_SIZE, feat).transpose(2, 0, 1, 3)
        return row.reshape(P_SIZE, groups, z_part * feat)

    early = jnp.concatenate([known(low_feature), known(mid_feature)], axis=-1)
    join_all = held(join_all)
    early, combine_table, block_in, join_all, returned = lax.optimization_barrier(
        (early, combine_table, block_in, join_all, returned)
    )
    sent = combine(accepted_node, combine_table, returned, block_in, early, P_SIZE * groups)
    spread = lax.all_to_all(sent, ("p", "y"), 0, 0, tiled=True)

    back = lax.all_to_all(join(spread, join_all), "p", 0, 0, tiled=True)
    return tuple(finish(back, (rows_dev, width), (trees, part)))


def solution(mesh):
    split = Mesh(mesh.devices.reshape(Z_SIZE, P_SIZE, -1), ("z", "p", "y"))
    every = ("z", "p", "y")
    placed = (
        P(every, None),
        P(),
        P(EXPERT, None),
        P(EXPERT, None),
        P(EXPERT, "y", None),
        P(EXPERT, "y", None),
        P(EXPERT, "y", None),
        P(every, None),
        P(every, None),
        P(EXPERT),
        P(None, EXPERT, "y"),
    )
    return jax.shard_map(
        on_device,
        mesh=split,
        in_specs=placed,
        out_specs=(P(every, None), P(EXPERT, "y")),
        check_vma=False,
    )
```

```python
import functools

import jax
import jax.numpy as jnp
from jax import lax
from jax.experimental import pallas as pl
from jax.experimental.pallas import tpu as pltpu
from jax.sharding import Mesh
from jax.sharding import PartitionSpec as P

EPSILON = 1e-06
Z_SIZE = 16
P_SIZE = 8
CAP = 4
EXPERT = ("z", "p")
F32 = jnp.float32
BF16 = jnp.bfloat16
PARAMS = pltpu.CompilerParams(vmem_limit_bytes=40 * 1024 * 1024)
VMEM = pl.BlockSpec(memory_space=pltpu.VMEM)
SMEM = pl.BlockSpec(memory_space=pltpu.SMEM)


def shift_y(array, groups, shift):
    return lax.ppermute(array, "y", [(j, (j + shift) % groups) for j in range(groups)])


def cost(flops, moved):
    return pl.CostEstimate(flops=flops, bytes_accessed=moved, transcendentals=0)


def norm_kernel(layer_ref, gain_ref, out_ref):
    groups, _, _, part = out_ref.shape
    widened = layer_ref[...].astype(F32)
    inverse = lax.rsqrt(jnp.mean(widened * widened, axis=-1, keepdims=True) + EPSILON)
    gain = gain_ref[...].reshape(1, -1).astype(F32)
    normed = (widened * inverse * gain).astype(BF16)
    for j in range(groups):
        out_ref[j, 0] = normed[:, j * part : (j + 1) * part]
        out_ref[j, 1] = layer_ref[:, j * part : (j + 1) * part]


def normed_and_raw(layer_in, norm_gain, groups):
    rows, width = layer_in.shape
    return pl.pallas_call(
        norm_kernel,
        out_shape=jax.ShapeDtypeStruct((groups, 2, rows, width // groups), BF16),
        in_specs=[VMEM] * 2,
        out_specs=VMEM,
        compiler_params=PARAMS,
        cost_estimate=cost(rows * width * 6, rows * width * 6),
        name="norm_pack",
    )(layer_in, norm_gain)


def slice_kernel(plan, groups, g_ref, *refs):
    sources, outs, sems = refs[:3], refs[3:-1], refs[-1]
    part = sources[0].shape[2] // groups
    copies = []
    for i, (out, moves) in enumerate(zip(outs, plan)):
        at = 0
        for k, (source, first, amount, shift) in enumerate(moves):
            lane = pl.multiple_of(lax.rem(g_ref[0] + shift, groups) * part, part)
            copies.append(
                pltpu.make_async_copy(
                    sources[source].at[0, pl.ds(first, amount), pl.ds(lane, part)],
                    out.at[pl.ds(at, amount), :],
                    sems.at[i, k],
                )
            )
            at += amount
    for copy in copies:
        copy.start()
    for copy in copies:
        copy.wait()


def weight_slices(g, sources, plan, groups, name, mib=60):
    part = sources[0].shape[2] // groups
    rows = [sum(amount for _, _, amount, _ in moves) for moves in plan]
    return pl.pallas_call(
        functools.partial(slice_kernel, plan, groups),
        out_shape=[jax.ShapeDtypeStruct((amount, part), BF16) for amount in rows],
        in_specs=[SMEM] + [pl.BlockSpec(memory_space=pltpu.HBM)] * 3,
        out_specs=[VMEM] * len(plan),
        scratch_shapes=[pltpu.SemaphoreType.DMA((len(plan), max(len(m) for m in plan)))],
        compiler_params=pltpu.CompilerParams(vmem_limit_bytes=mib * 1024 * 1024),
        cost_estimate=cost(0, 4 * sum(rows) * part),
        name=name,
    )(g, *sources)


def dispatch_kernel(table_ref, both_ref, out_ref):
    part = both_ref.shape[3]
    normed = both_ref[:, 0].reshape(-1, part)
    rows = dot_tn(table_ref[...], normed).astype(BF16)
    out_ref[...] = rows.reshape(out_ref.shape)


def dispatch_rows(table, both):
    part = both.shape[3]
    slots = table.shape[1]
    return pl.pallas_call(
        dispatch_kernel,
        out_shape=jax.ShapeDtypeStruct((slots // CAP, CAP, part), BF16),
        in_specs=[VMEM] * 2,
        out_specs=VMEM,
        compiler_params=PARAMS,
        cost_estimate=cost(2 * table.size * part, 2 * slots * part),
        name="dispatch",
    )(table, both)


def dot_nt(a, b):
    return lax.dot_general(a, b, (((1,), (1,)), ((), ())), preferred_element_type=F32)


def dot_tn(a, b):
    return lax.dot_general(a, b, (((0,), (0,)), ((), ())), preferred_element_type=F32)


def gate_up_kernel(groups, g_ref, rows_ref, *refs):
    pieces, out_ref = refs[:-1], refs[-1]
    rows = rows_ref[...].reshape(-1, rows_ref.shape[2])
    for s in range(groups):
        home = lax.rem(g_ref[0] + groups - s, groups)
        out_ref[home] = dot_nt(pieces[s][...], rows).astype(BF16)


def gate_up(g, rows, pieces):
    experts, cap, part = rows.shape
    slots = experts * cap
    groups = len(pieces)
    double = pieces[1].shape[0]
    return pl.pallas_call(
        functools.partial(gate_up_kernel, groups),
        out_shape=jax.ShapeDtypeStruct((groups, double, slots), BF16),
        grid_spec=pltpu.PrefetchScalarGridSpec(
            num_scalar_prefetch=1,
            grid=(1,),
            in_specs=[pl.BlockSpec(rows.shape, lambda i, g_ref: (0, 0, 0))]
            + [pl.BlockSpec((double, part), lambda i, g_ref: (0, 0))] * groups,
            out_specs=pl.BlockSpec((groups, double, slots), lambda i, g_ref: (0, 0, 0)),
        ),
        compiler_params=PARAMS,
        cost_estimate=cost(2 * slots * part * double * groups, 6 << 20),
        name="gate_up",
    )(g, rows, *pieces)


def silu_kernel(acts_ref, out_ref):
    units = out_ref.shape[0]
    gate = jnp.sum(acts_ref[:, :units].astype(F32), axis=0)
    up = jnp.sum(acts_ref[:, units:].astype(F32), axis=0)
    out_ref[...] = (gate / (1.0 + jnp.exp(-gate)) * up).astype(BF16)


def silu(acts):
    _, double, slots = acts.shape
    return pl.pallas_call(
        silu_kernel,
        out_shape=jax.ShapeDtypeStruct((double // 2, slots), BF16),
        in_specs=[VMEM],
        out_specs=VMEM,
        compiler_params=PARAMS,
        cost_estimate=cost(8 * double * slots, 2 << 20),
        name="silu_sum",
    )(acts)


def down_kernel(groups, g_ref, hidden_ref, *refs):
    pieces, out_ref = refs[:-1], refs[-1]
    units, part = pieces[0].shape
    experts, cap, _ = out_ref.shape
    g = g_ref[0]
    chunk = part // 4
    held = [
        hidden_ref[pl.ds(pl.multiple_of(lax.rem(g + groups - s, groups) * units, units), units), :]
        for s in range(groups)
    ]
    for n in range(4):
        columns = slice(n * chunk, (n + 1) * chunk)
        total = dot_tn(held[0], pieces[0][:, columns])
        for s in range(1, groups):
            total += dot_tn(held[s], pieces[s][:, columns])
        out_ref[:, :, columns] = total.astype(BF16).reshape(experts, cap, chunk)


def down(g, hidden, pieces):
    inner, slots = hidden.shape
    groups = len(pieces)
    units, part = inner // groups, pieces[0].shape[1]
    out = (slots // CAP, CAP, part)
    return pl.pallas_call(
        functools.partial(down_kernel, groups),
        out_shape=jax.ShapeDtypeStruct(out, BF16),
        grid_spec=pltpu.PrefetchScalarGridSpec(
            num_scalar_prefetch=1,
            grid=(1,),
            in_specs=[pl.BlockSpec((inner, slots), lambda i, g_ref: (0, 0))]
            + [
                pl.BlockSpec((units, part), lambda i, g_ref, k=piece.shape[0] // units - 1: (k, 0))
                for piece in pieces
            ],
            out_specs=pl.BlockSpec(out, lambda i, g_ref: (0, 0, 0)),
        ),
        compiler_params=PARAMS,
        cost_estimate=cost(2 * slots * inner * part, 4 << 20),
        name="down",
    )(g, hidden, *pieces)


def combine_kernel(node_ref, table_ref, returned_ref, block_ref, known_ref, out_ref):
    dests, trees, _ = out_ref.shape
    block, part = block_ref.shape
    peers = part // 128
    groups = dests // peers
    tree = block // trees
    zs = known_ref.shape[2] // 2 // 32
    returned = returned_ref[...].reshape(-1, part)
    moe = jnp.dot(table_ref[...], returned, preferred_element_type=F32)
    result = (block_ref[...].astype(F32) + moe).astype(BF16).astype(F32)
    place = lax.broadcasted_iota(jnp.int32, (tree, part), 0)
    chosen = []
    for t in range(trees):
        rows = result[t * tree : (t + 1) * tree]
        chosen.append(jnp.sum(jnp.where(place == node_ref[t], rows, 0.0), axis=0, keepdims=True))
    chosen = jnp.concatenate(chosen, axis=0)
    for p in range(peers):
        parts = [chosen[:, z * peers * 32 + p * 32 : z * peers * 32 + p * 32 + 32] for z in range(zs)]
        high = jnp.concatenate(parts, axis=1).astype(BF16)
        lanes = slice(p * 128, p * 128 + 128)
        for j in range(groups):
            d = p * groups + j
            out_ref[d, :, 0:256] = known_ref[p]
            out_ref[d, :, 256:384] = high
            rows = result[j * tree : (j + 1) * tree, lanes]
            out_ref[d, :, 384:512] = rows[:trees].astype(BF16)
            out_ref[d, :, 512:640] = rows[trees:].astype(BF16)


def combine(nodes, table, returned, block_in, known, dests):
    block, part = block_in.shape
    trees = nodes.shape[0]
    return pl.pallas_call(
        combine_kernel,
        out_shape=jax.ShapeDtypeStruct((dests, trees, 640), BF16),
        in_specs=[SMEM] + [VMEM] * 4,
        out_specs=VMEM,
        compiler_params=PARAMS,
        cost_estimate=cost(2 * block * table.shape[1] * part, 2 << 20),
        name="combine",
    )(nodes, table, returned, block_in, known)


def held_kernel(weight_ref, out_ref):
    out_ref[...] = weight_ref[...]


def held(weight):
    return pl.pallas_call(
        held_kernel,
        out_shape=jax.ShapeDtypeStruct(weight.shape, BF16),
        in_specs=[VMEM],
        out_specs=VMEM,
        compiler_params=PARAMS,
        cost_estimate=cost(0, 4 * weight.size),
        name="held",
    )(weight)


def join_kernel(rows_ref, tiles_ref, weight_ref, out_ref):
    amount, trees, step = tiles_ref.shape
    peers = out_ref.shape[0]
    line = 128
    quarter = weight_ref.shape[0] // trees
    high = jnp.concatenate(
        [rows_ref[:, t * step + 2 * line : t * step + 3 * line] for t in range(trees)], axis=0
    )
    row = lax.broadcasted_iota(jnp.int32, (amount, amount * trees), 0)
    column = lax.broadcasted_iota(jnp.int32, (amount, amount * trees), 1)
    place = lax.rem(column, amount)
    same = (lax.div(column, amount) == lax.rem(row, trees)) & (
        lax.div(place, trees) == lax.div(row, trees)
    )
    total = None
    for q in range(trees):
        chosen = jnp.where(same & (lax.rem(place, trees) == q), 1.0, 0.0).astype(BF16)
        parts = [
            rows_ref[:, q * step : q * step + line],
            rows_ref[:, q * step + line : q * step + 2 * line],
            jnp.dot(chosen, high, preferred_element_type=F32).astype(BF16),
        ]
        for k, values in enumerate(parts):
            weight = weight_ref[q * quarter : (q + 1) * quarter, k].reshape(line, -1)
            product = jnp.dot(values, weight, preferred_element_type=F32)
            total = product if total is None else total + product
    half = total.shape[1] // 2
    for p in range(peers):
        rows = slice(p * trees, (p + 1) * trees)
        pair = jnp.concatenate([total[rows, :half], total[rows, half:]], axis=0)
        out_ref[p, 0 : 2 * trees] = pair.astype(BF16)
        for j in range(trees):
            for h in range(2):
                lanes = slice((3 + h) * line, (4 + h) * line)
                out_ref[p, (2 + h) * trees : (3 + h) * trees, j * line : (j + 1) * line] = (
                    tiles_ref[p * trees + j, :, lanes]
                )


def join(tiles, weight):
    amount, trees, step = tiles.shape
    peers = amount // trees
    width = weight.shape[-1]
    return pl.pallas_call(
        join_kernel,
        out_shape=jax.ShapeDtypeStruct((peers, 4 * trees, width // 2), BF16),
        in_specs=[VMEM] * 3,
        out_specs=VMEM,
        compiler_params=PARAMS,
        cost_estimate=cost(2 * amount * weight.size, 4 << 20),
        name="join",
    )(tiles.reshape(amount, trees * step), tiles, weight)


def finish_kernel(back_ref, layer_ref, joined_ref):
    peers, rows, half = back_ref.shape
    trees = rows // 4
    summed = jnp.sum(back_ref[:, 0 : 2 * trees].astype(F32), axis=0)
    joined_ref[:, :half] = summed[:trees].astype(BF16)
    joined_ref[:, half:] = summed[trees:].astype(BF16)
    for p in range(peers):
        for j in range(trees):
            lane = j * 2 * half + p * 128
            layer_ref[:, lane : lane + 128] = back_ref[
                p, 2 * trees : 4 * trees, j * 128 : (j + 1) * 128
            ]


def finish(back, layer_shape, joined_shape):
    return pl.pallas_call(
        finish_kernel,
        out_shape=[
            jax.ShapeDtypeStruct(layer_shape, BF16),
            jax.ShapeDtypeStruct(joined_shape, BF16),
        ],
        in_specs=[VMEM],
        out_specs=[VMEM] * 2,
        compiler_params=PARAMS,
        cost_estimate=cost(back.size, back.size * 4),
        name="finish",
    )(back)


def route_weights(route_logits):
    exponent = jnp.exp(route_logits)
    return (exponent / jnp.sum(exponent, axis=-1, keepdims=True)).astype(BF16)


def slot_places(route_ids, experts):
    flat_ids = route_ids.reshape(-1)
    amount = flat_ids.shape[0]
    onehot = flat_ids[:, None] == jnp.arange(experts, dtype=jnp.int32)[None, :]
    lower = jnp.arange(amount)[:, None] > jnp.arange(amount)[None, :]
    before = jnp.dot(lower.astype(BF16), onehot.astype(BF16), preferred_element_type=F32)
    rank = jnp.sum(jnp.where(onehot, before, 0.0), axis=1).astype(jnp.int32)
    return flat_ids * CAP + rank


def on_device(
    layer_in,
    norm_gain,
    route_ids,
    route_logits,
    gate_proj,
    up_proj,
    down_proj,
    low_feature,
    mid_feature,
    accepted_node,
    join_weight,
):
    groups = lax.axis_size("y")
    experts = Z_SIZE * P_SIZE
    g = lax.axis_index("y").astype(jnp.int32)
    g_one = g.reshape(1)
    rows_dev, width = layer_in.shape
    block, top = route_ids.shape
    part = width // groups
    slots = experts * CAP
    trees = accepted_node.shape[0]

    join_all = lax.all_gather(join_weight, "z", axis=0, tiled=False)

    both = normed_and_raw(layer_in, norm_gain, groups)
    both = lax.all_to_all(both, "y", 0, 0, tiled=True)
    block_in = both[:, 1].reshape(block, part)

    weights = route_weights(route_logits)
    places = slot_places(route_ids, experts)
    slot_ids = jnp.arange(slots, dtype=jnp.int32)
    matches = (places[:, None] == slot_ids[None, :]).reshape(block, top, slots)
    dispatch = jnp.any(matches, axis=1).astype(BF16)
    outgoing = dispatch_rows(dispatch, both)

    units = gate_proj.shape[1]
    sources = [gate_proj, up_proj, down_proj]

    def plan(shift, kinds):
        return [(kind, 0, units, shift) for kind in kinds]

    cut = [plan(1, (0, 1)), plan(2, (0, 1, 2)), plan(3, (0, 1))]
    cut = weight_slices(g_one, sources, cut, groups, "first_slices")
    outgoing, *cut = lax.optimization_barrier((outgoing, *cut))
    near = [shift_y(cut[0], groups, 1), shift_y(cut[2], groups, 3)]
    far = shift_y(cut[1], groups, 2)
    cut = weight_slices(g_one, sources, [plan(1, (2,)), plan(3, (2,))], groups, "down_slices")
    near_down = [shift_y(cut[0], groups, 1), shift_y(cut[1], groups, 3)]
    (own,) = weight_slices(g_one, sources, [plan(0, (0, 1, 2))], groups, "own_slices", 40)
    gate_up_pieces = [own, near[0], far, near[1]]
    down_pieces = [own, near_down[0], far, near_down[1]]
    received = lax.all_to_all(outgoing, EXPERT, 0, 0, tiled=True)

    combine_table = jnp.sum(
        jnp.where(matches, weights.astype(F32)[:, :, None], 0.0), axis=1
    ).astype(BF16)

    acts = gate_up(g_one, received, gate_up_pieces)
    acts, down_pieces[1], down_pieces[3] = lax.optimization_barrier(
        (acts, down_pieces[1], down_pieces[3])
    )
    acts = lax.all_to_all(acts, "y", 0, 0, tiled=True)
    hidden = silu(acts)
    hidden_all = lax.all_gather(hidden, "y", axis=0, tiled=True)
    expert_out = down(g_one, hidden_all, down_pieces)
    returned = lax.all_to_all(expert_out, EXPERT, 0, 0, tiled=True)

    own_node = lax.dynamic_slice_in_dim(accepted_node, g, 1, 0)[0]
    feat = width // experts
    z_part = Z_SIZE // groups

    def known(feature):
        row = lax.dynamic_index_in_dim(feature, own_node, 0, keepdims=False)
        row = row.reshape(groups, z_part, P_SIZE, feat).transpose(2, 0, 1, 3)
        return row.reshape(P_SIZE, groups, z_part * feat)

    early = jnp.concatenate([known(low_feature), known(mid_feature)], axis=-1)
    join_all = held(join_all)
    early, combine_table, block_in, join_all, returned = lax.optimization_barrier(
        (early, combine_table, block_in, join_all, returned)
    )
    sent = combine(accepted_node, combine_table, returned, block_in, early, P_SIZE * groups)
    spread = lax.all_to_all(sent, ("p", "y"), 0, 0, tiled=True)

    back = lax.all_to_all(join(spread, join_all), "p", 0, 0, tiled=True)
    return tuple(finish(back, (rows_dev, width), (trees, part)))


def solution(mesh):
    split = Mesh(mesh.devices.reshape(Z_SIZE, P_SIZE, -1), ("z", "p", "y"))
    every = ("z", "p", "y")
    placed = (
        P(every, None),
        P(),
        P(EXPERT, None),
        P(EXPERT, None),
        P(EXPERT, "y", None),
        P(EXPERT, "y", None),
        P(EXPERT, "y", None),
        P(every, None),
        P(every, None),
        P(EXPERT),
        P(None, EXPERT, "y"),
    )
    return jax.shard_map(
        on_device,
        mesh=split,
        in_specs=placed,
        out_specs=(P(every, None), P(EXPERT, "y")),
        check_vma=False,
    )
```
